32 devices in a mesh: dom: 8 (over y, x, core), rep: 4 (over z).
Axes of the slice: x: 2, y: 2, z: 4, core: 2. Of those that a mesh axis runs over, the one named last changes fastest.
Arguments:
- features: bfloat16 [8192, 256], P(('dom', 'rep')), may hold values from -6 to 6
- degree: int32 [8192], P(('dom', 'rep')), may hold values from 1 to 64
- tile_row: int32 [8, 8, 4], P('dom', 'rep'), may hold values from 0 to 7, as said below
- tile_col: int32 [8, 8, 4], P('dom', 'rep'), may hold values from 0 to 7, as said below
- tile_count: int32 [8, 8, 4, 128, 128], P('dom', 'rep'), may hold values from 0 to 3, as said below
- tile_live: int32 [8, 8], P('dom', 'rep'), may hold values from 1 to 4, as said below
- weight: bfloat16 [256, 256], replicated, may hold values from -0.375 to 0.375
- bias: float32 [256], replicated, may hold values from -3 to 3
- cotangent: bfloat16 [8192, 256], P(('dom', 'rep'))
Outputs:
- activation: bfloat16 [8192, 256], P(('dom', 'rep'))
- weight_grad: float32 [256, 256], replicated
- bias_grad: float32 [256], replicated
The draws below stay inside these ranges and needn't reach their ends.
Inputs may be any that keep to these rules, and one draw needn't show every extreme that they name: `tile_live`: the number of live slots of partition d at section s; in every draw some partition has all 4 slots live at every section. `tile_row`: live slots of one partition and section name distinct (row, column) tile pairs; two live slots may share a row, and their products add up; slots at or past tile_live hold 0. `tile_col`: slots at or past tile_live hold 0. `tile_count`: tiles of slots at or past tile_live are zero.
All inputs are finite; a program needn't handle non-finite values.
Results may differ from the reference program's by a relative error of at most 0.015.
Values may be sent and summed in bfloat16 or wider, within the bound.
No kernel may reach another device: no remote copies, remote signals or barrier semaphores. Data moves between devices by JAX's collectives and lax.ppermute only.
A program may use at most 64 MiB of HBM per device.

```python
import math
import jax
import jax.numpy as jnp
from jax import lax

F = 256
BLOCK = 128
ROWS = 256
TS = 4
BPD = 8
NODES = 8192
N_DOM = 8
N_REP = 4


def live_table(key):
    sub = jax.random.fold_in(key, 202)
    first, second, third = jax.random.split(sub, 3)
    heavy = jax.random.randint(first, (N_DOM,), 0, 8) == 0
    forced = jax.random.randint(second, (), 0, N_DOM)
    heavy = heavy | (jnp.arange(N_DOM) == forced)
    light = jax.random.randint(third, (N_DOM, N_DOM), 1, max(TS // 2, 1) + 1)
    return jnp.where(heavy[:, None], TS, light).astype(jnp.int32)


def pair_table(key):
    live_count = live_table(key)
    sub = jax.random.fold_in(key, 303)
    keys = jax.random.split(sub, N_DOM * N_DOM)
    picks = jax.vmap(lambda single: jax.random.permutation(single, BPD * BPD)[:TS])(keys)
    picks = picks.reshape(N_DOM, N_DOM, TS)
    active = jnp.arange(TS)[None, None, :] < live_count[:, :, None]
    return jnp.where(active, picks, 0).astype(jnp.int32)


def draw_tile_live(key, part):
    return live_table(key)


def draw_tile_row(key, part):
    pairs = pair_table(key)
    return (pairs // BPD).astype(jnp.int32)


def draw_tile_col(key, part):
    pairs = pair_table(key)
    return (pairs % BPD).astype(jnp.int32)


def draw_tile_count(key, part):
    live_count = live_table(key)
    key = jax.random.fold_in(key, 7)
    first, second = jax.random.split(key)
    shape = (N_DOM, N_DOM, TS, BLOCK, BLOCK)
    present = jax.random.randint(first, shape, 0, 4) == 0
    values = jax.random.randint(second, shape, 1, 4)
    active = jnp.arange(TS)[None, None, :] < live_count[:, :, None]
    keep = present & active[:, :, :, None, None]
    return jnp.where(keep, values, 0).astype(jnp.int32)


def draw_cotangent(key, part):
    key = jax.random.fold_in(key, 5)
    first = jax.random.fold_in(key, 0)
    position = jnp.arange(NODES, dtype=jnp.float32) / NODES
    row_scale = jnp.exp(math.log(3.0) * position) * NODES ** (-0.5)
    base = jax.random.normal(first, (NODES, F), jnp.float32)
    return (row_scale[:, None] * base).astype(jnp.bfloat16)


def place_ends(result, own_key, low, high):
    longest = result.shape.index(max(result.shape))
    spots = []
    for shift in (0, 1):
        where = [jax.random.randint(jax.random.fold_in(own_key, axis), (), 0, length) for axis, length in enumerate(result.shape)]
        where[longest] = (where[longest] + shift) % result.shape[longest]
        spots.append(tuple(where))
    return result.at[spots[0]].set(low).at[spots[1]].set(high)


def steps_of(key, extent, cuts, smallest, high):
    factor_of = 1.0
    for axis_at, shards_of in cuts:
        draws = jax.random.uniform(jax.random.fold_in(jax.random.fold_in(key, 6), axis_at), (shards_of,), jnp.float32, smallest / len(cuts), high / len(cuts))
        factor_of = factor_of * jnp.repeat(jnp.exp(draws), extent[axis_at] // shards_of).reshape((-1,) + (1,) * (len(extent) - 1 - axis_at))
    return factor_of


def scatter_about(own_key, extent, deviation, bound, shards=(), held_as=jnp.bfloat16):
    drawn = jax.random.normal(own_key, extent, jnp.float32) * deviation
    if len(shards) > 0:
        drawn = steps_of(own_key, extent, shards, -0.22, 0.18) * drawn
    return jnp.clip(drawn, min=-bound, max=bound).astype(held_as)


def setup_inputs(seed: int = 0) -> dict:
    key_list = jax.random.split(jax.random.key(seed), 10)
    return {
        "features": scatter_about(key_list[0], (NODES, F), 1.0, 6.0, ((0, 32),)),
        "degree": place_ends(jax.random.randint(key_list[1], (NODES,), 1, 65), jax.random.fold_in(key_list[1], 1), 1, 64).astype(jnp.int32),
        "tile_row": draw_tile_row(jax.random.fold_in(key_list[9], 71), 0),
        "tile_col": draw_tile_col(jax.random.fold_in(key_list[9], 71), 0),
        "tile_count": draw_tile_count(jax.random.fold_in(key_list[9], 71), 0),
        "tile_live": draw_tile_live(jax.random.fold_in(key_list[9], 71), 0),
        "weight": scatter_about(key_list[6], (F, F), F ** -0.5, 0.375),
        "bias": scatter_about(key_list[7], (F,), 0.5, 3.0, (), jnp.float32),
        "cotangent": draw_cotangent(jax.random.fold_in(key_list[9], 71), 0),
    }


def smooth(values):
    return jax.nn.gelu(values, approximate=True)

def reference(features, degree, tile_row, tile_col, tile_count, tile_live, weight, bias, cotangent):
    inv_root = lax.rsqrt(degree.astype(jnp.float32))
    scaled = (features.astype(jnp.float32) * inv_root[:, None]).astype(jnp.bfloat16)
    block_count = N_REP * ROWS // BLOCK
    blocks = scaled.reshape(N_DOM, block_count, BLOCK, F)

    def one_dom(dom_idx):

        def over_section(totals, section_idx):

            def one_slot(slot_idx, inner):
                edge_tile = tile_count[dom_idx, section_idx, slot_idx].astype(jnp.float32)
                col_block = blocks[section_idx, tile_col[dom_idx, section_idx, slot_idx]].astype(jnp.float32)
                product = jnp.dot(edge_tile, col_block, precision=lax.Precision.HIGHEST, preferred_element_type=jnp.float32)
                row_idx = tile_row[dom_idx, section_idx, slot_idx].astype(jnp.int32)
                current = lax.dynamic_index_in_dim(inner, row_idx, 0, keepdims=False)
                return lax.dynamic_update_index_in_dim(inner, current + product, row_idx, 0)
            live_count = tile_live[dom_idx, section_idx].astype(jnp.int32)
            return (lax.fori_loop(jnp.int32(0), live_count, one_slot, totals), None)
        start = jnp.zeros((block_count, BLOCK, F), jnp.float32)
        totals, unused = lax.scan(over_section, start, jnp.arange(N_DOM, dtype=jnp.int32))
        return totals
    agg = lax.map(one_dom, jnp.arange(N_DOM, dtype=jnp.int32)).reshape(NODES, F)
    mixed = ((agg + scaled.astype(jnp.float32)) * inv_root[:, None]).astype(jnp.bfloat16)
    pre = jnp.dot(mixed, weight, preferred_element_type=jnp.float32) + bias
    outcome, pull = jax.vjp(smooth, pre)
    slope = pull(cotangent.astype(jnp.float32))[0]
    slope_b = slope.astype(jnp.bfloat16)
    weight_grad = jnp.dot(mixed.T, slope_b, preferred_element_type=jnp.float32)
    bias_grad = lax.optimization_barrier(jnp.sum(slope, axis=0))
    return (outcome.astype(jnp.bfloat16), weight_grad, bias_grad)
```

```python
import jax
import jax.numpy as jnp
from jax import lax
from jax.experimental import pallas as pl
from jax.experimental.pallas import tpu as pltpu
from jax.sharding import PartitionSpec as P

VMEM = pl.BlockSpec(memory_space=pltpu.VMEM)
SMEM = pl.BlockSpec(memory_space=pltpu.SMEM)
PARAMS = pltpu.CompilerParams(vmem_limit_bytes=48 * 1024 * 1024)
GELU_C = 0.7978845608028654


def column_of(row, width):
    return jnp.transpose(jnp.broadcast_to(row, (width, row.shape[1])))


def scale_kernel(features_ref, degree_ref, out_ref):
    width = features_ref.shape[1]
    inv_root = column_of(lax.rsqrt(degree_ref[...].astype(jnp.float32)), 128)
    for at in range(0, width, 128):
        part = features_ref[:, at : at + 128].astype(jnp.float32)
        out_ref[:, at : at + 128] = (part * inv_root).astype(jnp.bfloat16)


def aggregate_kernel(dom_size, rep_size, *refs):
    row_ref, col_ref, count_ref = refs[:3]
    piece_refs = refs[3 : 3 + dom_size]
    out_ref, held, acc = refs[3 + dom_size :]
    sections, slots, block = count_ref.shape[1], count_ref.shape[2], count_ref.shape[3]
    per_piece = piece_refs[0].shape[0] // block
    for mask, piece_ref in enumerate(piece_refs):
        for half in range(per_piece):
            held[mask * per_piece + half] = piece_ref[half * block : (half + 1) * block, :]
    acc[...] = jnp.zeros_like(acc)
    dom, rep = lax.axis_index("dom"), lax.axis_index("rep")

    def slot_step(at):
        section, slot = at // slots, at % slots
        col = col_ref[0, section, slot]
        source = ((col // per_piece) ^ rep) * sections + section
        rows = held[(source ^ dom) * per_piece + col % per_piece]
        tile = count_ref[0, section, slot].astype(jnp.float32).astype(jnp.bfloat16)
        acc[row_ref[0, section, slot]] += jnp.dot(
            tile, rows, preferred_element_type=jnp.float32
        )

    if sections * slots <= 8:
        for at in range(sections * slots):
            slot_step(at)
    else:
        lax.fori_loop(0, sections * slots, lambda at, c: (slot_step(at), c)[1], 0)
    out_ref[...] = acc[...].astype(jnp.bfloat16)


def dense_kernel(
    parts_ref, scaled_ref, degree_ref, weight_ref, bias_ref, cotangent_ref,
    out_ref, keep_ref, send_ref,
):
    rep_size, row_count, width = parts_ref.shape
    inv_root = column_of(lax.rsqrt(degree_ref[...].astype(jnp.float32)), 128)
    inv_root = jnp.concatenate([inv_root] * (width // 128), axis=1)
    agg = parts_ref[0].astype(jnp.float32)
    for at in range(1, rep_size):
        agg += parts_ref[at].astype(jnp.float32)
    mixed = ((agg + scaled_ref[...].astype(jnp.float32)) * inv_root).astype(jnp.bfloat16)
    pre = jnp.dot(mixed, weight_ref[...], preferred_element_type=jnp.float32) + bias_ref[...]
    square = pre * pre
    bent = jnp.tanh(GELU_C * (pre + 0.044715 * (square * pre)))
    half = 0.5 * (1.0 + bent)
    out_ref[...] = (pre * half).astype(jnp.bfloat16)
    inner = GELU_C * (1.0 + (3 * 0.044715) * square)
    slope = cotangent_ref[...].astype(jnp.float32) * (
        half + 0.5 * pre * ((1.0 - bent) * (1.0 + bent)) * inner
    )
    weight_term = lax.dot_general(
        mixed, slope.astype(jnp.bfloat16), (((0,), (0,)), ((), ())),
        preferred_element_type=jnp.float32,
    )
    bias_term = jnp.sum(slope, axis=0, keepdims=True)
    kept = width // 2
    top, bottom = weight_term[:kept], weight_term[kept:]
    core = lax.axis_index("dom") % 2
    keep_ref[:kept, :] = jnp.where(core == 0, top, bottom)
    send_ref[:kept, :] = jnp.where(core == 0, bottom, top)
    extra = jnp.broadcast_to(bias_term, (keep_ref.shape[0] - kept, width))
    keep_ref[kept:, :] = extra
    send_ref[kept:, :] = extra


def xor_pairs(size, mask):
    return [(at, at ^ mask) for at in range(size)]


def exchange_sum(value, axis, masks):
    size = lax.axis_size(axis)
    while masks:
        now, masks = masks[:2], masks[2:]
        first = lax.ppermute(value, axis, xor_pairs(size, now[0]))
        if len(now) == 1:
            total = value.astype(jnp.float32) + first.astype(jnp.float32)
        else:
            second = lax.ppermute(value, axis, xor_pairs(size, now[1]))
            third = lax.ppermute(value, axis, xor_pairs(size, now[0] ^ now[1]))
            total = (value.astype(jnp.float32) + first.astype(jnp.float32)) + (
                second.astype(jnp.float32) + third.astype(jnp.float32)
            )
        value = total.astype(value.dtype)
    return value


def bits_of(size):
    return [1 << at for at in range(size.bit_length() - 1)]


def on_device(features, degree, tile_row, tile_col, tile_count, tile_live, weight, bias, cotangent):
    row_count, width = features.shape
    dom_size, rep_size = lax.axis_size("dom"), lax.axis_size("rep")
    sections, slots, block = tile_count.shape[1], tile_count.shape[2], tile_count.shape[3]
    block_count = row_count * rep_size // block
    degree_row = degree.reshape(1, row_count)
    shard = jax.ShapeDtypeStruct((row_count, width), jnp.bfloat16)

    scaled = pl.pallas_call(
        scale_kernel, out_shape=shard, in_specs=[VMEM, VMEM], out_specs=VMEM, name="scale"
    )(features, degree_row)

    moves = []
    for dom in range(dom_size):
        for rep in range(rep_size):
            target = ((dom // sections) ^ rep) * sections + dom % sections
            moves.append((dom * rep_size + rep, target * rep_size + dom // sections))
    piece = lax.ppermute(scaled, ("dom", "rep"), moves)

    pieces = [None] * dom_size
    pieces[0] = piece
    for mask in range(2, dom_size, 2):
        pieces[mask] = lax.ppermute(piece, "dom", xor_pairs(dom_size, mask))
    for mask in range(0, dom_size, 2):
        pieces[mask + 1] = lax.ppermute(pieces[mask], "dom", xor_pairs(dom_size, 1))

    partial = pl.pallas_call(
        lambda *refs: aggregate_kernel(dom_size, rep_size, *refs),
        out_shape=jax.ShapeDtypeStruct((block_count, block, width), jnp.bfloat16),
        in_specs=[SMEM, SMEM, VMEM] + [VMEM] * dom_size,
        out_specs=VMEM,
        scratch_shapes=[
            pltpu.VMEM((dom_size * row_count // block, block, width), jnp.bfloat16),
            pltpu.VMEM((block_count, block, width), jnp.float32),
        ],
        compiler_params=PARAMS,
        name="aggregate",
    )(tile_row, tile_col, tile_count, *pieces)

    parts = lax.all_to_all(partial.reshape(rep_size, row_count, width), "rep", 0, 0)

    half = jax.ShapeDtypeStruct((width // 2 + 8, width), jnp.float32)
    outcome, keep, send = pl.pallas_call(
        dense_kernel,
        out_shape=(shard, half, half),
        in_specs=[VMEM] * 6,
        out_specs=(VMEM,) * 3,
        compiler_params=PARAMS,
        name="dense",
    )(parts, scaled, degree_row, weight, bias.reshape(1, width), cotangent)

    swap = xor_pairs(dom_size, 1)
    mine = (keep + lax.ppermute(send, "dom", swap)).astype(jnp.bfloat16)
    mine = exchange_sum(mine, "dom", bits_of(dom_size)[1:])
    mine = exchange_sum(mine, "rep", bits_of(rep_size))
    other = lax.ppermute(mine, "dom", swap)
    kept = width // 2
    first = lax.axis_index("dom") % 2 == 0
    top = jnp.where(first, mine, other)
    bottom = jnp.where(first, other, mine)
    weight_grad = jnp.concatenate([top[:kept], bottom[:kept]], axis=0).astype(jnp.float32)
    bias_grad = top[kept].astype(jnp.float32)
    return (outcome, weight_grad, bias_grad)


def solution(mesh):
    return jax.shard_map(
        on_device,
        mesh=mesh,
        in_specs=(
            P(("dom", "rep"), None),
            P(("dom", "rep")),
            P("dom", "rep", None),
            P("dom", "rep", None),
            P("dom", "rep", None, None, None),
            P("dom", "rep"),
            P(),
            P(),
            P(("dom", "rep"), None),
        ),
        out_specs=(P(("dom", "rep"), None), P(), P()),
        check_vma=False,
    )
```

```python
import jax
import jax.numpy as jnp
from jax import lax
from jax.experimental import pallas as pl
from jax.experimental.pallas import tpu as pltpu
from jax.sharding import PartitionSpec as P

VMEM = pl.BlockSpec(memory_space=pltpu.VMEM)
SMEM = pl.BlockSpec(memory_space=pltpu.SMEM)
PARAMS = pltpu.CompilerParams(vmem_limit_bytes=32 * 1024 * 1024)
GELU_C = 0.7978845608028654


LATIN = ((1, 0, 2, 3), (3, 2, 0, 1), (0, 1, 3, 2), (2, 3, 1, 0))
LATIN_BITS = sum(
    to << (2 * (4 * plane + rep)) for plane, row in enumerate(LATIN) for rep, to in enumerate(row)
)


def chip_of(plane, rep, rep_size):
    if rep_size != 4:
        return plane ^ rep
    if isinstance(plane, int):
        return LATIN[plane][rep]
    bits = jnp.int32(LATIN_BITS - (1 << 32) if LATIN_BITS >> 31 else LATIN_BITS)
    return lax.shift_right_logical(bits, 2 * (4 * plane + rep)) & 3


def column_of(row, width):
    return jnp.transpose(jnp.broadcast_to(row, (width, row.shape[1])))


def scale_kernel(sections, features_ref, degree_ref, *out_refs):
    width = features_ref.shape[1] // 2
    inv_root = column_of(lax.rsqrt(degree_ref[...].astype(jnp.float32)), width)
    halves = []
    for half in range(2):
        part = features_ref[:, half * width : (half + 1) * width].astype(jnp.float32)
        halves.append((part * inv_root).astype(jnp.bfloat16))
    odd = (lax.axis_index("dom") // sections) % 2
    for out_ref, first, second in zip(out_refs, halves, halves[::-1]):
        out_ref[...] = jnp.where(odd == 0, first, second)


def cast_kernel(count_ref, out_ref):
    out_ref[...] = count_ref[0].reshape(out_ref.shape).astype(jnp.float32).astype(jnp.bfloat16)


def join_kernel(first_ref, second_ref, out_ref):
    rows = first_ref.shape[0]
    out_ref[:rows, :] = first_ref[...]
    out_ref[rows:, :] = second_ref[...]


def aggregate_kernel(dom_size, rep_size, sections, *refs):
    code_refs, tile_refs, refs = refs[:2], refs[2:4], refs[4:]
    piece_refs, refs = refs[:dom_size], refs[dom_size:]
    out_refs, (held, acc) = refs[:rep_size], refs[rep_size:]
    slots, block = tile_refs[0].shape[0] // sections, tile_refs[0].shape[1]
    block_count = acc.shape[0]
    per_piece = piece_refs[0].shape[0] // block
    per_slice = per_piece // 2
    for mask, piece_ref in enumerate(piece_refs):
        for at in range(per_piece):
            held[mask * per_piece + at] = piece_ref[at * block : (at + 1) * block, :]
    acc[...] = jnp.zeros_like(acc)
    dom, rep = lax.axis_index("dom"), lax.axis_index("rep")

    for which in range(2):
        code_ref, tile_ref = code_refs[which], tile_refs[which]

        def slot_step(at):
            section, slot = at // slots, at % slots
            code = code_ref[0, section, slot]
            row, col = code // block_count, code % block_count
            chip = chip_of(rep ^ which, col // per_slice, rep_size)
            mask = (chip * sections + section) ^ dom
            rows = held[mask * per_piece + which * per_slice + col % per_slice]
            acc[row] += jnp.dot(tile_ref[at], rows, preferred_element_type=jnp.float32)

        if sections * slots <= 8:
            for at in range(sections * slots):
                slot_step(at)
        else:
            lax.fori_loop(0, sections * slots, lambda at, c: (slot_step(at), c)[1], 0)

    for mask, out_ref in enumerate(out_refs):
        for at in range(per_slice):
            part = acc[(rep ^ mask) * per_slice + at]
            out_ref[at * block : (at + 1) * block, :] = part.astype(jnp.bfloat16)


def dense_kernel(rep_size, *refs):
    part_refs, refs = refs[:rep_size], refs[rep_size:]
    features_ref, degree_ref, weight_ref, bias_ref, cotangent_ref, out_ref, keep_ref, send_ref = refs
    width = features_ref.shape[1]
    inv_root = column_of(lax.rsqrt(degree_ref[...].astype(jnp.float32)), width // 2)
    inv_root = jnp.concatenate([inv_root, inv_root], axis=1)
    sums = [0.0, 0.0]
    for mask, part_ref in enumerate(part_refs):
        sums[mask % 2] += part_ref[...].astype(jnp.float32)
    odd = lax.axis_index("rep") % 2
    agg = jnp.concatenate(
        [jnp.where(odd == 0, sums[0], sums[1]), jnp.where(odd == 0, sums[1], sums[0])], axis=1
    )
    scaled = (features_ref[...].astype(jnp.float32) * inv_root).astype(jnp.bfloat16)
    mixed = ((agg + scaled.astype(jnp.float32)) * inv_root).astype(jnp.bfloat16)
    pre = jnp.dot(mixed, weight_ref[...], preferred_element_type=jnp.float32) + bias_ref[...]
    square = pre * pre
    bent = jnp.tanh(GELU_C * (pre + 0.044715 * (square * pre)))
    half = 0.5 * (1.0 + bent)
    out_ref[...] = (pre * half).astype(jnp.bfloat16)
    inner = GELU_C * (1.0 + (3 * 0.044715) * square)
    slope = cotangent_ref[...].astype(jnp.float32) * (
        half + 0.5 * pre * ((1.0 - bent) * (1.0 + bent)) * inner
    )
    weight_term = lax.dot_general(
        mixed, slope.astype(jnp.bfloat16), (((0,), (0,)), ((), ())),
        preferred_element_type=jnp.float32,
    )
    bias_term = jnp.sum(slope, axis=0, keepdims=True)
    kept = width // 2
    top, bottom = weight_term[:kept], weight_term[kept:]
    core = lax.axis_index("dom") % 2
    keep_ref[:kept, :] = jnp.where(core == 0, top, bottom)
    send_ref[:kept, :] = jnp.where(core == 0, bottom, top)
    extra = jnp.broadcast_to(bias_term, (keep_ref.shape[0] - kept, width))
    keep_ref[kept:, :] = extra
    send_ref[kept:, :] = extra


def finish_kernel(mine_ref, other_ref, weight_ref, bias_ref):
    kept = weight_ref.shape[0] // 2
    first = lax.axis_index("dom") % 2 == 0
    mine = mine_ref[...].astype(jnp.float32)
    other = other_ref[...].astype(jnp.float32)
    weight_ref[:kept, :] = jnp.where(first, mine[:kept], other[:kept])
    weight_ref[kept:, :] = jnp.where(first, other[:kept], mine[:kept])
    bias_ref[...] = mine[kept : kept + 1]


def xor_pairs(size, mask):
    return [(at, at ^ mask) for at in range(size)]


def exchange_sum(value, axis, masks):
    size = lax.axis_size(axis)
    while masks:
        now, masks = masks[:2], masks[2:]
        first = lax.ppermute(value, axis, xor_pairs(size, now[0]))
        if len(now) == 1:
            total = value.astype(jnp.float32) + first.astype(jnp.float32)
        else:
            second = lax.ppermute(value, axis, xor_pairs(size, now[1]))
            third = lax.ppermute(value, axis, xor_pairs(size, now[0] ^ now[1]))
            total = (value.astype(jnp.float32) + first.astype(jnp.float32)) + (
                second.astype(jnp.float32) + third.astype(jnp.float32)
            )
        value = total.astype(value.dtype)
    return value


def bits_of(size):
    return [1 << at for at in range(size.bit_length() - 1)]


def on_device(features, degree, tile_row, tile_col, tile_count, tile_live, weight, bias, cotangent):
    row_count, width = features.shape
    dom_size, rep_size = lax.axis_size("dom"), lax.axis_size("rep")
    sections, slots, block = tile_count.shape[1], tile_count.shape[2], tile_count.shape[3]
    block_count = row_count * rep_size // block
    degree_row = degree.reshape(1, row_count)
    bf16, f32 = jnp.bfloat16, jnp.float32
    half = jax.ShapeDtypeStruct((row_count, width // 2), bf16)

    outgoing = pl.pallas_call(
        lambda *refs: scale_kernel(sections, *refs),
        out_shape=(half, half), in_specs=[VMEM, VMEM], out_specs=(VMEM, VMEM), name="scale",
    )(features, degree_row)
    arrived = []
    for flip, part in enumerate(outgoing):
        moves = []
        for dom in range(dom_size):
            plane = dom // sections
            for rep in range(rep_size):
                target = chip_of(plane, rep, rep_size) * sections + dom % sections
                moves.append((dom * rep_size + rep, target * rep_size + (plane ^ flip)))
        arrived.append(lax.ppermute(part, ("dom", "rep"), moves))

    tiles = pl.pallas_call(
        cast_kernel,
        out_shape=jax.ShapeDtypeStruct((sections * slots, block, block), bf16),
        in_specs=[VMEM], out_specs=VMEM, compiler_params=PARAMS, name="cast",
    )(tile_count)
    codes = tile_row * block_count + tile_col
    pair = xor_pairs(rep_size, 1)
    their_codes = lax.ppermute(codes, "rep", pair)
    their_tiles = lax.ppermute(tiles, "rep", pair)

    pieces = [None] * dom_size
    pieces[0] = pl.pallas_call(
        join_kernel,
        out_shape=jax.ShapeDtypeStruct((2 * row_count, width // 2), bf16),
        in_specs=[VMEM, VMEM], out_specs=VMEM, name="join",
    )(*arrived)
    for mask in range(2, dom_size, 2):
        pieces[mask] = lax.ppermute(pieces[0], "dom", xor_pairs(dom_size, mask))
    for mask in range(0, dom_size, 2):
        pieces[mask + 1] = lax.ppermute(pieces[mask], "dom", xor_pairs(dom_size, 1))

    held_shape = (dom_size * 2 * row_count // block, block, width // 2)
    partials = pl.pallas_call(
        lambda *refs: aggregate_kernel(dom_size, rep_size, sections, *refs),
        out_shape=(half,) * rep_size,
        in_specs=[SMEM, SMEM] + [VMEM] * (2 + dom_size),
        out_specs=(VMEM,) * rep_size,
        scratch_shapes=[
            pltpu.VMEM(held_shape, bf16),
            pltpu.VMEM((block_count, block, width // 2), f32),
        ],
        compiler_params=PARAMS,
        name="aggregate",
    )(codes, their_codes, tiles, their_tiles, *pieces)

    parts = [partials[0]]
    for mask in range(1, rep_size):
        parts.append(lax.ppermute(partials[mask], "rep", xor_pairs(rep_size, mask)))

    share = jax.ShapeDtypeStruct((width // 2 + 16, width), f32)
    outcome, keep, send = pl.pallas_call(
        lambda *refs: dense_kernel(rep_size, *refs),
        out_shape=(jax.ShapeDtypeStruct((row_count, width), bf16), share, share),
        in_specs=[VMEM] * (rep_size + 5),
        out_specs=(VMEM,) * 3,
        compiler_params=PARAMS,
        name="dense",
    )(*parts, features, degree_row, weight, bias.reshape(1, width), cotangent)

    swap = xor_pairs(dom_size, 1)
    mine = (keep + lax.ppermute(send, "dom", swap)).astype(bf16)
    mine = exchange_sum(mine, "dom", bits_of(dom_size)[1:])
    mine = exchange_sum(mine, "rep", bits_of(rep_size))
    other = lax.ppermute(mine, "dom", swap)
    weight_grad, bias_grad = pl.pallas_call(
        finish_kernel,
        out_shape=(
            jax.ShapeDtypeStruct((width, width), f32), jax.ShapeDtypeStruct((1, width), f32),
        ),
        in_specs=[VMEM, VMEM], out_specs=(VMEM, VMEM), name="finish",
    )(mine, other)
    return (outcome, weight_grad, bias_grad.reshape(width))


def solution(mesh):
    return jax.shard_map(
        on_device,
        mesh=mesh,
        in_specs=(
            P(("dom", "rep"), None),
            P(("dom", "rep")),
            P("dom", "rep", None),
            P("dom", "rep", None),
            P("dom", "rep", None, None, None),
            P("dom", "rep"),
            P(),
            P(),
            P(("dom", "rep"), None),
        ),
        out_specs=(P(("dom", "rep"), None), P(), P()),
        check_vma=False,
    )
```

```python
import math

import jax
import jax.numpy as jnp
from jax import lax
from jax.experimental import pallas as pl
from jax.experimental.pallas import tpu as pltpu
from jax.sharding import PartitionSpec as P

VMEM = pl.BlockSpec(memory_space=pltpu.VMEM)
SMEM = pl.BlockSpec(memory_space=pltpu.SMEM)
GELU_C = 0.7978845608028654


LATIN = ((1, 0, 2, 3), (3, 2, 0, 1), (0, 1, 3, 2), (2, 3, 1, 0))
LATIN_BITS = sum(
    to << (2 * (4 * plane + rep)) for plane, row in enumerate(LATIN) for rep, to in enumerate(row)
)


def chip_of(plane, rep, rep_size):
    if rep_size != 4:
        return plane ^ rep
    if isinstance(plane, int):
        return LATIN[plane][rep]
    bits = jnp.int32(LATIN_BITS - (1 << 32) if LATIN_BITS >> 31 else LATIN_BITS)
    return lax.shift_right_logical(bits, 2 * (4 * plane + rep)) & 3


def local_call(kernel, name, inputs, in_specs, out_shape, scratch=()):
    size = sum(
        math.prod(each.shape) * each.dtype.itemsize
        for each in (*inputs, *jax.tree.leaves(out_shape), *scratch)
    )
    return pl.pallas_call(
        kernel,
        out_shape=out_shape,
        in_specs=in_specs,
        out_specs=jax.tree.map(lambda each: SMEM if each.dtype == jnp.int32 else VMEM, out_shape),
        scratch_shapes=[pltpu.VMEM(each.shape, each.dtype) for each in scratch],
        compiler_params=pltpu.CompilerParams(vmem_limit_bytes=size + 4 * 1024 * 1024),
        name=name,
    )(*inputs)


def column_of(row, width):
    return jnp.transpose(jnp.broadcast_to(row, (width, row.shape[1])))


def scale_kernel(sections, features_ref, degree_ref, *out_refs):
    width = features_ref.shape[1] // 2
    inv_root = column_of(lax.rsqrt(degree_ref[...].astype(jnp.float32)), width)
    halves = []
    for half in range(2):
        part = features_ref[:, half * width : (half + 1) * width].astype(jnp.float32)
        halves.append((part * inv_root).astype(jnp.bfloat16))
    odd = (lax.axis_index("dom") // sections) % 2
    for out_ref, first, second in zip(out_refs, halves, halves[::-1]):
        out_ref[...] = jnp.where(odd == 0, first, second)


def prepare_kernel(
    block_count, count_ref, row_ref, col_ref, features_ref, degree_ref,
    tiles_ref, codes_ref, scaled_ref, inv_ref,
):
    tiles_ref[...] = count_ref[0].reshape(tiles_ref.shape).astype(jnp.float32).astype(jnp.bfloat16)
    sections, slots = codes_ref.shape[1:]

    def code_step(at, carry):
        section, slot = at // slots, at % slots
        code = row_ref[0, section, slot] * block_count + col_ref[0, section, slot]
        codes_ref[0, section, slot] = code
        return carry

    lax.fori_loop(0, sections * slots, code_step, 0)
    width = inv_ref.shape[1]
    inv_root = column_of(lax.rsqrt(degree_ref[...].astype(jnp.float32)), width)
    inv_ref[...] = inv_root
    for at in range(0, features_ref.shape[1], width):
        part = features_ref[:, at : at + width].astype(jnp.float32)
        scaled_ref[:, at : at + width] = (part * inv_root).astype(jnp.bfloat16)


def join_kernel(first_ref, second_ref, out_ref):
    rows = first_ref.shape[0]
    out_ref[:rows, :] = first_ref[...]
    out_ref[rows:, :] = second_ref[...]


def aggregate_kernel(dom_size, rep_size, sections, *refs):
    code_refs, tile_refs, refs = refs[:2], refs[2:4], refs[4:]
    piece_refs, refs = refs[:dom_size], refs[dom_size:]
    out_refs, (held, acc) = refs[:rep_size], refs[rep_size:]
    slots, block = tile_refs[0].shape[0] // sections, tile_refs[0].shape[1]
    block_count = acc.shape[0]
    per_piece = piece_refs[0].shape[0] // block
    per_slice = per_piece // 2
    for mask, piece_ref in enumerate(piece_refs):
        for at in range(per_piece):
            held[mask * per_piece + at] = piece_ref[at * block : (at + 1) * block, :]
    acc[...] = jnp.zeros_like(acc)
    dom, rep = lax.axis_index("dom"), lax.axis_index("rep")

    for which in range(2):
        code_ref, tile_ref = code_refs[which], tile_refs[which]

        def slot_step(at):
            section, slot = at // slots, at % slots
            code = code_ref[0, section, slot]
            row, col = code // block_count, code % block_count
            chip = chip_of(rep ^ which, col // per_slice, rep_size)
            mask = (chip * sections + section) ^ dom
            rows = held[mask * per_piece + which * per_slice + col % per_slice]
            acc[row] += jnp.dot(tile_ref[at], rows, preferred_element_type=jnp.float32)

        if sections * slots <= 8:
            for at in range(sections * slots):
                slot_step(at)
        else:
            lax.fori_loop(0, sections * slots, lambda at, c: (slot_step(at), c)[1], 0)

    for mask, out_ref in enumerate(out_refs):
        for at in range(per_slice):
            part = acc[(rep ^ mask) * per_slice + at]
            out_ref[at * block : (at + 1) * block, :] = part.astype(jnp.bfloat16)


def dense_kernel(rep_size, *refs):
    part_refs, refs = refs[:rep_size], refs[rep_size:]
    scaled_ref, inv_ref, weight_ref, bias_ref, cotangent_ref, out_ref, keep_ref, send_ref = refs
    width = scaled_ref.shape[1]
    inv_root = jnp.concatenate([inv_ref[...]] * 2, axis=1)
    sums = [0.0, 0.0]
    for mask, part_ref in enumerate(part_refs):
        sums[mask % 2] += part_ref[...].astype(jnp.float32)
    odd = lax.axis_index("rep") % 2
    agg = jnp.concatenate(
        [jnp.where(odd == 0, sums[0], sums[1]), jnp.where(odd == 0, sums[1], sums[0])], axis=1
    )
    mixed = ((agg + scaled_ref[...].astype(jnp.float32)) * inv_root).astype(jnp.bfloat16)
    pre = jnp.dot(mixed, weight_ref[...], preferred_element_type=jnp.float32) + bias_ref[...]
    square = pre * pre
    bent = jnp.tanh(GELU_C * (pre + 0.044715 * (square * pre)))
    half = 0.5 * (1.0 + bent)
    out_ref[...] = (pre * half).astype(jnp.bfloat16)
    inner = GELU_C * (1.0 + (3 * 0.044715) * square)
    slope = cotangent_ref[...].astype(jnp.float32) * (
        half + 0.5 * pre * ((1.0 - bent) * (1.0 + bent)) * inner
    )
    weight_term = lax.dot_general(
        mixed, slope.astype(jnp.bfloat16), (((0,), (0,)), ((), ())),
        preferred_element_type=jnp.float32,
    )
    bias_term = jnp.sum(slope, axis=0, keepdims=True)
    kept = width // 2
    top, bottom = weight_term[:kept], weight_term[kept:]
    core = lax.axis_index("dom") % 2
    keep_ref[:kept, :] = jnp.where(core == 0, top, bottom)
    send_ref[:kept, :] = jnp.where(core == 0, bottom, top)
    extra = jnp.broadcast_to(bias_term, (keep_ref.shape[0] - kept, width))
    keep_ref[kept:, :] = extra
    send_ref[kept:, :] = extra


def finish_kernel(mine_ref, other_ref, weight_ref, bias_ref):
    kept = weight_ref.shape[0] // 2
    first = lax.axis_index("dom") % 2 == 0
    mine = mine_ref[...].astype(jnp.float32)
    other = other_ref[...].astype(jnp.float32)
    weight_ref[:kept, :] = jnp.where(first, mine[:kept], other[:kept])
    weight_ref[kept:, :] = jnp.where(first, other[:kept], mine[:kept])
    bias_ref[...] = mine[kept : kept + 1]


def xor_pairs(size, mask):
    return [(at, at ^ mask) for at in range(size)]


def exchange_sum(value, axis, masks):
    size = lax.axis_size(axis)
    while masks:
        now, masks = masks[:2], masks[2:]
        first = lax.ppermute(value, axis, xor_pairs(size, now[0]))
        if len(now) == 1:
            total = value.astype(jnp.float32) + first.astype(jnp.float32)
        else:
            second = lax.ppermute(value, axis, xor_pairs(size, now[1]))
            third = lax.ppermute(value, axis, xor_pairs(size, now[0] ^ now[1]))
            total = (value.astype(jnp.float32) + first.astype(jnp.float32)) + (
                second.astype(jnp.float32) + third.astype(jnp.float32)
            )
        value = total.astype(value.dtype)
    return value


def bits_of(size):
    return [1 << at for at in range(size.bit_length() - 1)]


def on_device(features, degree, tile_row, tile_col, tile_count, tile_live, weight, bias, cotangent):
    row_count, width = features.shape
    dom_size, rep_size = lax.axis_size("dom"), lax.axis_size("rep")
    sections, slots, block = tile_count.shape[1], tile_count.shape[2], tile_count.shape[3]
    block_count = row_count * rep_size // block
    degree_row = degree.reshape(1, row_count)
    bf16, f32 = jnp.bfloat16, jnp.float32
    half = jax.ShapeDtypeStruct((row_count, width // 2), bf16)

    outgoing = local_call(
        lambda *refs: scale_kernel(sections, *refs), "scale",
        (features, degree_row), [VMEM] * 2, (half, half),
    )
    arrived = []
    for flip, part in enumerate(outgoing):
        moves = []
        for dom in range(dom_size):
            plane = dom // sections
            for rep in range(rep_size):
                target = chip_of(plane, rep, rep_size) * sections + dom % sections
                moves.append((dom * rep_size + rep, target * rep_size + (plane ^ flip)))
        arrived.append(lax.ppermute(part, ("dom", "rep"), moves))

    tiles, codes, scaled, inv_root = local_call(
        lambda *refs: prepare_kernel(block_count, *refs), "prepare",
        (tile_count, tile_row, tile_col, features, degree_row), [VMEM, SMEM, SMEM, VMEM, VMEM],
        (
            jax.ShapeDtypeStruct((sections * slots, block, block), bf16),
            jax.ShapeDtypeStruct(tile_row.shape, jnp.int32),
            jax.ShapeDtypeStruct((row_count, width), bf16),
            jax.ShapeDtypeStruct((row_count, width // 2), f32),
        ),
    )
    pair = xor_pairs(rep_size, 1)
    their_codes = lax.ppermute(codes, "rep", pair)
    their_tiles = lax.ppermute(tiles, "rep", pair)
    arrived, their_codes = lax.optimization_barrier((arrived, their_codes))

    pieces = [None] * dom_size
    pieces[0] = local_call(
        join_kernel, "join", arrived, [VMEM] * 2,
        jax.ShapeDtypeStruct((2 * row_count, width // 2), bf16),
    )
    for mask in range(2, dom_size, 2):
        pieces[mask] = lax.ppermute(pieces[0], "dom", xor_pairs(dom_size, mask))
    for mask in range(0, dom_size, 2):
        pieces[mask + 1] = lax.ppermute(pieces[mask], "dom", xor_pairs(dom_size, 1))

    partials = local_call(
        lambda *refs: aggregate_kernel(dom_size, rep_size, sections, *refs), "aggregate",
        (codes, their_codes, tiles, their_tiles, *pieces), [SMEM] * 2 + [VMEM] * (2 + dom_size),
        (half,) * rep_size,
        (
            jax.ShapeDtypeStruct((dom_size * 2 * row_count // block, block, width // 2), bf16),
            jax.ShapeDtypeStruct((block_count, block, width // 2), f32),
        ),
    )

    parts = [partials[0]]
    for mask in range(1, rep_size):
        parts.append(lax.ppermute(partials[mask], "rep", xor_pairs(rep_size, mask)))

    share = jax.ShapeDtypeStruct((width // 2 + 16, width), f32)
    outcome, keep, send = local_call(
        lambda *refs: dense_kernel(rep_size, *refs), "dense",
        (*parts, scaled, inv_root, weight, bias.reshape(1, width), cotangent),
        [VMEM] * (rep_size + 5),
        (jax.ShapeDtypeStruct((row_count, width), bf16), share, share),
    )

    swap = xor_pairs(dom_size, 1)
    mine = (keep + lax.ppermute(send, "dom", swap)).astype(bf16)
    mine = exchange_sum(mine, "dom", bits_of(dom_size)[1:])
    mine = exchange_sum(mine, "rep", bits_of(rep_size))
    other = lax.ppermute(mine, "dom", swap)
    weight_grad, bias_grad = local_call(
        finish_kernel, "finish", (mine, other), [VMEM] * 2,
        (jax.ShapeDtypeStruct((width, width), f32), jax.ShapeDtypeStruct((1, width), f32)),
    )
    return (outcome, weight_grad, bias_grad.reshape(width))


def solution(mesh):
    return jax.shard_map(
        on_device,
        mesh=mesh,
        in_specs=(
            P(("dom", "rep"), None),
            P(("dom", "rep")),
            P("dom", "rep", None),
            P("dom", "rep", None),
            P("dom", "rep", None, None, None),
            P("dom", "rep"),
            P(),
            P(),
            P(("dom", "rep"), None),
        ),
        out_specs=(P(("dom", "rep"), None), P(), P()),
        check_vma=False,
    )
```

```python
import math

import jax
import jax.numpy as jnp
from jax import lax
from jax.experimental import pallas as pl
from jax.experimental.pallas import tpu as pltpu
from jax.sharding import PartitionSpec as P

VMEM = pl.BlockSpec(memory_space=pltpu.VMEM)
SMEM = pl.BlockSpec(memory_space=pltpu.SMEM)
HBM = pl.BlockSpec(memory_space=pltpu.MemorySpace.HBM)
CODE_ROWS = 16
GELU_C = 0.7978845608028654


ASIDE = ((3, 1, 2, 0), (1, 3, 2, 0), (0, 1, 3, 2), (0, 2, 1, 3))
ASIDE_BITS = sum(
    to << (2 * (4 * plane + rep)) for plane, row in enumerate(ASIDE) for rep, to in enumerate(row)
)


def chip_of(source, plane, rep, rep_size):
    if rep_size != 4:
        return source ^ rep
    if isinstance(plane, int):
        return source ^ ASIDE[plane][rep]
    bits = jnp.int32(ASIDE_BITS - (1 << 32) if ASIDE_BITS >> 31 else ASIDE_BITS)
    return source ^ (lax.shift_right_logical(bits, 2 * (4 * plane + rep)) & 3)


def local_call(kernel, name, inputs, in_specs, out_shape, scratch=(), small=(), spare=4):
    size = sum(
        math.prod(each.shape) * each.dtype.itemsize
        for each in (*inputs, *jax.tree.leaves(out_shape), *scratch)
    )
    return pl.pallas_call(
        kernel,
        out_shape=out_shape,
        in_specs=in_specs,
        out_specs=jax.tree.map(lambda each: VMEM, out_shape),
        scratch_shapes=[pltpu.VMEM(each.shape, each.dtype) for each in scratch] + list(small),
        compiler_params=pltpu.CompilerParams(vmem_limit_bytes=size + spare * 1024 * 1024),
        name=name,
    )(*inputs)


def column_of(row, width):
    return jnp.transpose(jnp.broadcast_to(row, (width, row.shape[1])))


def scale_kernel(sections, features_hbm, degree_hbm, *refs):
    out_refs, (features_ref, degree_ref, sems) = refs[:2], refs[2:]
    copies = [
        pltpu.make_async_copy(degree_hbm, degree_ref, sems.at[0]),
        pltpu.make_async_copy(features_hbm, features_ref, sems.at[1]),
    ]
    for copy in copies:
        copy.start()
    copies[0].wait()
    width = features_ref.shape[1] // 2
    inv_root = column_of(lax.rsqrt(degree_ref[...].astype(jnp.float32)), width)
    copies[1].wait()
    halves = []
    for half in range(2):
        part = features_ref[:, half * width : (half + 1) * width].astype(jnp.float32)
        halves.append((part * inv_root).astype(jnp.bfloat16))
    odd = (lax.axis_index("dom") // sections) % 2
    for out_ref, first, second in zip(out_refs, halves, halves[::-1]):
        out_ref[...] = jnp.where(odd == 0, first, second)


def prepare_kernel(
    block_count, count_ref, row_ref, col_ref, features_ref, degree_ref, bias_ref,
    tiles_ref, scaled_ref, inv_ref, bias_out_ref,
):
    _, sections, slots, block, _ = count_ref.shape
    for at in range(sections * slots):
        tile = count_ref[0, at // slots, at % slots].astype(jnp.float32)
        tiles_ref[at * block : (at + 1) * block, :] = tile.astype(jnp.bfloat16)
    lane = lax.broadcasted_iota(jnp.int32, (CODE_ROWS, block), 1)

    def code_step(at, codes):
        section, slot = at // slots, at % slots
        code = row_ref[0, section, slot] * block_count + col_ref[0, section, slot]
        return jnp.where(lane == at, code, codes)

    codes = lax.fori_loop(0, sections * slots, code_step, jnp.zeros_like(lane))
    tiles_ref[sections * slots * block :, :] = codes.astype(jnp.float32).astype(jnp.bfloat16)
    width = inv_ref.shape[1]
    inv_root = column_of(lax.rsqrt(degree_ref[...].astype(jnp.float32)), width)
    inv_ref[...] = inv_root
    for at in range(0, features_ref.shape[1], width):
        part = features_ref[:, at : at + width].astype(jnp.float32)
        scaled_ref[:, at : at + width] = (part * inv_root).astype(jnp.bfloat16)
    bias_out_ref[...] = bias_ref[...]


def join_kernel(first_ref, second_ref, out_ref):
    rows = first_ref.shape[0]
    out_ref[:rows, :] = first_ref[...]
    out_ref[rows:, :] = second_ref[...]


def aggregate_kernel(dom_size, rep_size, sections, slots, *refs):
    row_ref, col_ref, *tile_refs = refs[:4]
    piece_refs, refs = refs[4 : 4 + dom_size], refs[4 + dom_size :]
    out_refs, (held, acc) = refs[:rep_size], refs[rep_size:]
    block = tile_refs[0].shape[1]
    tile_rows = sections * slots * block
    block_count = acc.shape[0]
    per_piece = piece_refs[0].shape[0] // block
    per_slice = per_piece // 2
    code_rows = tile_refs[1][tile_rows:, :].astype(jnp.float32)
    lane = lax.broadcasted_iota(jnp.int32, code_rows.shape, 1)
    dom, rep = lax.axis_index("dom"), lax.axis_index("rep")

    def code_of(at):
        return jnp.max(jnp.where(lane == at, code_rows, 0.0)).astype(jnp.int32)

    def add_slot(which, at, row, col):
        chip = chip_of(rep ^ which, rep, col // per_slice, rep_size)
        mask = (chip * sections + at // slots) ^ dom
        rows = held[mask * per_piece + which * per_slice + col % per_slice]
        tile = tile_refs[which][pl.ds(at * block, block), :]
        acc[row] += jnp.dot(tile, rows, preferred_element_type=jnp.float32)

    def own_step(at, carry):
        section, slot = at // slots, at % slots
        add_slot(0, at, row_ref[0, section, slot], col_ref[0, section, slot])
        return carry

    def their_step(at, carry):
        code = code_of(at)
        add_slot(1, at, code // block_count, code % block_count)
        return carry

    few = sections * slots <= 8
    codes = [code_of(at) for at in range(sections * slots)] if few else None
    for mask, piece_ref in enumerate(piece_refs):
        for at in range(per_piece):
            held[mask * per_piece + at] = piece_ref[at * block : (at + 1) * block, :]
    acc[...] = jnp.zeros_like(acc)
    lax.fori_loop(0, sections * slots, own_step, 0, unroll=few)
    if few:
        for at, code in enumerate(codes):
            add_slot(1, at, code // block_count, code % block_count)
    else:
        lax.fori_loop(0, sections * slots, their_step, 0)

    for mask, out_ref in enumerate(out_refs):
        for at in range(per_slice):
            part = acc[(rep ^ mask) * per_slice + at]
            out_ref[at * block : (at + 1) * block, :] = part.astype(jnp.bfloat16)


def dense_kernel(rep_size, *refs):
    part_refs, refs = refs[:rep_size], refs[rep_size:]
    scaled_ref, inv_ref, weight_ref, bias_ref, cotangent_ref, out_ref, keep_ref, send_ref = refs
    width = scaled_ref.shape[1]
    inv_root = jnp.concatenate([inv_ref[...]] * 2, axis=1)
    sums = [0.0, 0.0]
    for mask, part_ref in enumerate(part_refs):
        sums[mask % 2] += part_ref[...].astype(jnp.float32)
    odd = lax.axis_index("rep") % 2
    agg = jnp.concatenate(
        [jnp.where(odd == 0, sums[0], sums[1]), jnp.where(odd == 0, sums[1], sums[0])], axis=1
    )
    mixed = ((agg + scaled_ref[...].astype(jnp.float32)) * inv_root).astype(jnp.bfloat16)
    pre = jnp.dot(mixed, weight_ref[...], preferred_element_type=jnp.float32) + bias_ref[...]
    square = pre * pre
    bent = jnp.tanh(GELU_C * (pre + 0.044715 * (square * pre)))
    half = 0.5 * (1.0 + bent)
    out_ref[...] = (pre * half).astype(jnp.bfloat16)
    inner = GELU_C * (1.0 + (3 * 0.044715) * square)
    slope = cotangent_ref[...].astype(jnp.float32) * (
        half + 0.5 * pre * ((1.0 - bent) * (1.0 + bent)) * inner
    )
    weight_term = lax.dot_general(
        mixed, slope.astype(jnp.bfloat16), (((0,), (0,)), ((), ())),
        preferred_element_type=jnp.float32,
    )
    bias_term = jnp.sum(slope, axis=0, keepdims=True)
    kept = width // 2
    top, bottom = weight_term[:kept], weight_term[kept:]
    core = lax.axis_index("dom") % 2
    keep_ref[:kept, :] = jnp.where(core == 0, top, bottom)
    send_ref[:kept, :] = jnp.where(core == 0, bottom, top)
    extra = jnp.broadcast_to(bias_term, (keep_ref.shape[0] - kept, width))
    keep_ref[kept:, :] = extra
    send_ref[kept:, :] = extra


def finish_kernel(mine_ref, other_ref, weight_ref, bias_ref):
    kept = weight_ref.shape[0] // 2
    first = lax.axis_index("dom") % 2 == 0
    mine = mine_ref[...].astype(jnp.float32)
    other = other_ref[...].astype(jnp.float32)
    weight_ref[:kept, :] = jnp.where(first, mine[:kept], other[:kept])
    weight_ref[kept:, :] = jnp.where(first, other[:kept], mine[:kept])
    bias_ref[...] = mine[kept : kept + 1]


def xor_pairs(size, mask):
    return [(at, at ^ mask) for at in range(size)]


def exchange_sum(value, axis, masks):
    size = lax.axis_size(axis)
    while masks:
        now, masks = masks[:2], masks[2:]
        first = lax.ppermute(value, axis, xor_pairs(size, now[0]))
        if len(now) == 1:
            total = value.astype(jnp.float32) + first.astype(jnp.float32)
        else:
            second = lax.ppermute(value, axis, xor_pairs(size, now[1]))
            third = lax.ppermute(value, axis, xor_pairs(size, now[0] ^ now[1]))
            total = (value.astype(jnp.float32) + first.astype(jnp.float32)) + (
                second.astype(jnp.float32) + third.astype(jnp.float32)
            )
        value = total.astype(value.dtype)
    return value


def bits_of(size):
    return [1 << at for at in range(size.bit_length() - 1)]


def on_device(features, degree, tile_row, tile_col, tile_count, tile_live, weight, bias, cotangent):
    row_count, width = features.shape
    dom_size, rep_size = lax.axis_size("dom"), lax.axis_size("rep")
    sections, slots, block = tile_count.shape[1], tile_count.shape[2], tile_count.shape[3]
    block_count = row_count * rep_size // block
    degree_row = degree.reshape(1, row_count)
    bf16, f32 = jnp.bfloat16, jnp.float32
    half = jax.ShapeDtypeStruct((row_count, width // 2), bf16)

    outgoing = local_call(
        lambda *refs: scale_kernel(sections, *refs), "scale",
        (features, degree_row), [HBM] * 2, (half, half), (features, degree_row),
        [pltpu.SemaphoreType.DMA((2,))], 58,
    )
    arrived = []
    for flip, part in enumerate(outgoing):
        moves = []
        for dom in range(dom_size):
            plane = dom // sections
            for rep in range(rep_size):
                target = chip_of(plane, plane ^ flip, rep, rep_size) * sections + dom % sections
                moves.append((dom * rep_size + rep, target * rep_size + (plane ^ flip)))
        arrived.append(lax.ppermute(part, ("dom", "rep"), moves))

    tiles, scaled, inv_root, bias_row = local_call(
        lambda *refs: prepare_kernel(block_count, *refs), "prepare",
        (tile_count, tile_row, tile_col, features, degree_row, bias.reshape(1, width)),
        [VMEM, SMEM, SMEM, VMEM, VMEM, VMEM],
        (
            jax.ShapeDtypeStruct((sections * slots * block + CODE_ROWS, block), bf16),
            jax.ShapeDtypeStruct((row_count, width), bf16),
            jax.ShapeDtypeStruct((row_count, width // 2), f32),
            jax.ShapeDtypeStruct((1, width), f32),
        ),
    )
    their_tiles = lax.ppermute(tiles, "rep", xor_pairs(rep_size, 1))

    pieces = [None] * dom_size
    pieces[0] = local_call(
        join_kernel, "join", arrived, [VMEM] * 2,
        jax.ShapeDtypeStruct((2 * row_count, width // 2), bf16),
    )
    for mask in range(2, dom_size, 2):
        pieces[mask] = lax.ppermute(pieces[0], "dom", xor_pairs(dom_size, mask))
    for mask in range(0, dom_size, 2):
        pieces[mask + 1] = lax.ppermute(pieces[mask], "dom", xor_pairs(dom_size, 1))

    partials = local_call(
        lambda *refs: aggregate_kernel(dom_size, rep_size, sections, slots, *refs), "aggregate",
        (tile_row, tile_col, tiles, their_tiles, *pieces), [SMEM] * 2 + [VMEM] * (2 + dom_size),
        (half,) * rep_size,
        (
            jax.ShapeDtypeStruct((dom_size * 2 * row_count // block, block, width // 2), bf16),
            jax.ShapeDtypeStruct((block_count, block, width // 2), f32),
        ),
    )

    parts = [partials[0]]
    for mask in range(1, rep_size):
        parts.append(lax.ppermute(partials[mask], "rep", xor_pairs(rep_size, mask)))

    share = jax.ShapeDtypeStruct((width // 2 + 16, width), f32)
    outcome, keep, send = local_call(
        lambda *refs: dense_kernel(rep_size, *refs), "dense",
        (*parts, scaled, inv_root, weight, bias_row, cotangent),
        [VMEM] * (rep_size + 5),
        (jax.ShapeDtypeStruct((row_count, width), bf16), share, share),
    )

    swap = xor_pairs(dom_size, 1)
    mine = (keep + lax.ppermute(send, "dom", swap)).astype(bf16)
    mine = exchange_sum(mine, "dom", bits_of(dom_size)[1:])
    mine = exchange_sum(mine, "rep", bits_of(rep_size))
    other = lax.ppermute(mine, "dom", swap)
    weight_grad, bias_grad = local_call(
        finish_kernel, "finish", (mine, other), [VMEM] * 2,
        (jax.ShapeDtypeStruct((width, width), f32), jax.ShapeDtypeStruct((1, width), f32)),
    )
    return (outcome, weight_grad, bias_grad.reshape(width))


def solution(mesh):
    return jax.shard_map(
        on_device,
        mesh=mesh,
        in_specs=(
            P(("dom", "rep"), None),
            P(("dom", "rep")),
            P("dom", "rep", None),
            P("dom", "rep", None),
            P("dom", "rep", None, None, None),
            P("dom", "rep"),
            P(),
            P(),
            P(("dom", "rep"), None),
        ),
        out_specs=(P(("dom", "rep"), None), P(), P()),
        check_vma=False,
    )
```

```python
import math

import jax
import jax.numpy as jnp
from jax import lax
from jax.experimental import pallas as pl
from jax.experimental.pallas import tpu as pltpu
from jax.sharding import PartitionSpec as P

VMEM = pl.BlockSpec(memory_space=pltpu.VMEM)
SMEM = pl.BlockSpec(memory_space=pltpu.SMEM)
HBM = pl.BlockSpec(memory_space=pltpu.MemorySpace.HBM)
CODE_ROWS = 16
GELU_C = 0.7978845608028654


ASIDE = ((3, 1, 2, 0), (1, 3, 2, 0), (0, 1, 3, 2), (0, 2, 1, 3))
ASIDE_BITS = sum(
    to << (2 * (4 * plane + rep)) for plane, row in enumerate(ASIDE) for rep, to in enumerate(row)
)


def chip_of(source, plane, rep, rep_size):
    if rep_size != 4:
        return source ^ rep
    if isinstance(plane, int):
        return source ^ ASIDE[plane][rep]
    bits = jnp.int32(ASIDE_BITS - (1 << 32) if ASIDE_BITS >> 31 else ASIDE_BITS)
    return source ^ (lax.shift_right_logical(bits, 2 * (4 * plane + rep)) & 3)


def local_call(kernel, name, inputs, in_specs, out_shape, scratch=(), small=(), spare=4):
    size = sum(
        math.prod(each.shape) * each.dtype.itemsize
        for each in (*inputs, *jax.tree.leaves(out_shape), *scratch)
    )
    return pl.pallas_call(
        kernel,
        out_shape=out_shape,
        in_specs=in_specs,
        out_specs=jax.tree.map(lambda each: VMEM, out_shape),
        scratch_shapes=[pltpu.VMEM(each.shape, each.dtype) for each in scratch] + list(small),
        compiler_params=pltpu.CompilerParams(vmem_limit_bytes=size + spare * 1024 * 1024),
        name=name,
    )(*inputs)


def column_of(row, width):
    return jnp.transpose(jnp.broadcast_to(row, (width, row.shape[1])))


def scale_kernel(sections, features_hbm, degree_hbm, *refs):
    out_refs, (features_ref, degree_ref, sems) = refs[:2], refs[2:]
    copies = [
        pltpu.make_async_copy(degree_hbm, degree_ref, sems.at[0]),
        pltpu.make_async_copy(features_hbm, features_ref, sems.at[1]),
    ]
    for copy in copies:
        copy.start()
    copies[0].wait()
    width = features_ref.shape[1] // 2
    inv_root = column_of(lax.rsqrt(degree_ref[...].astype(jnp.float32)), width)
    copies[1].wait()
    halves = []
    for half in range(2):
        part = features_ref[:, half * width : (half + 1) * width].astype(jnp.float32)
        halves.append((part * inv_root).astype(jnp.bfloat16))
    odd = (lax.axis_index("dom") // sections) % 2
    for out_ref, first, second in zip(out_refs, halves, halves[::-1]):
        out_ref[...] = jnp.where(odd == 0, first, second)


def prepare_kernel(
    block_count, count_ref, row_ref, col_ref, features_ref, degree_ref, bias_ref,
    tiles_ref, scaled_ref, inv_ref, bias_out_ref,
):
    _, sections, slots, block, _ = count_ref.shape
    for at in range(sections * slots):
        tile = count_ref[0, at // slots, at % slots].astype(jnp.float32)
        tiles_ref[at * block : (at + 1) * block, :] = tile.astype(jnp.bfloat16)
    lane = lax.broadcasted_iota(jnp.int32, (CODE_ROWS, block), 1)

    def code_step(at, codes):
        section, slot = at // slots, at % slots
        code = row_ref[0, section, slot] * block_count + col_ref[0, section, slot]
        return jnp.where(lane == at, code, codes)

    codes = lax.fori_loop(0, sections * slots, code_step, jnp.zeros_like(lane))
    tiles_ref[sections * slots * block :, :] = codes.astype(jnp.float32).astype(jnp.bfloat16)
    width = inv_ref.shape[1]
    inv_root = column_of(lax.rsqrt(degree_ref[...].astype(jnp.float32)), width)
    inv_ref[...] = inv_root
    for at in range(0, features_ref.shape[1], width):
        part = features_ref[:, at : at + width].astype(jnp.float32)
        scaled_ref[:, at : at + width] = (part * inv_root).astype(jnp.bfloat16)
    bias_out_ref[...] = bias_ref[...]


def join_kernel(first_ref, second_ref, out_ref):
    rows = first_ref.shape[0]
    out_ref[:rows, :] = first_ref[...]
    out_ref[rows:, :] = second_ref[...]


def aggregate_kernel(dom_size, rep_size, sections, slots, *refs):
    tile_refs, refs = refs[:2], refs[2:]
    piece_refs, refs = refs[:dom_size], refs[dom_size:]
    out_refs, (held, acc) = refs[:rep_size], refs[rep_size:]
    block = tile_refs[0].shape[1]
    tile_rows = sections * slots * block
    block_count = acc.shape[0]
    per_piece = piece_refs[0].shape[0] // block
    per_slice = per_piece // 2
    code_rows = [tile_ref[tile_rows:, :].astype(jnp.float32) for tile_ref in tile_refs]
    lane = lax.broadcasted_iota(jnp.int32, code_rows[0].shape, 1)
    dom, rep = lax.axis_index("dom"), lax.axis_index("rep")

    def code_of(which, at):
        return jnp.max(jnp.where(lane == at, code_rows[which], 0.0)).astype(jnp.int32)

    def add_slot(which, at, code):
        row, col = code // block_count, code % block_count
        chip = chip_of(rep ^ which, rep, col // per_slice, rep_size)
        mask = (chip * sections + at // slots) ^ dom
        rows = held[mask * per_piece + which * per_slice + col % per_slice]
        tile = tile_refs[which][pl.ds(at * block, block), :]
        acc[row] += jnp.dot(tile, rows, preferred_element_type=jnp.float32)

    def both_step(at, carry):
        for which in range(2):
            add_slot(which, at, code_of(which, at))
        return carry

    few = sections * slots <= 8
    order = [(which, at) for which in range(2) for at in range(sections * slots)]
    codes = [code_of(*each) for each in order] if few else None
    for mask, piece_ref in enumerate(piece_refs):
        for at in range(per_piece):
            held[mask * per_piece + at] = piece_ref[at * block : (at + 1) * block, :]
    acc[...] = jnp.zeros_like(acc)
    if few:
        for (which, at), code in zip(order, codes):
            add_slot(which, at, code)
    else:
        lax.fori_loop(0, sections * slots, both_step, 0)

    for mask, out_ref in enumerate(out_refs):
        for at in range(per_slice):
            part = acc[(rep ^ mask) * per_slice + at]
            out_ref[at * block : (at + 1) * block, :] = part.astype(jnp.bfloat16)


def dense_kernel(rep_size, *refs):
    part_refs, refs = refs[:rep_size], refs[rep_size:]
    scaled_ref, inv_ref, weight_ref, bias_ref, cotangent_ref, out_ref, keep_ref, send_ref = refs
    width = scaled_ref.shape[1]
    inv_root = jnp.concatenate([inv_ref[...]] * 2, axis=1)
    sums = [0.0, 0.0]
    for mask, part_ref in enumerate(part_refs):
        sums[mask % 2] += part_ref[...].astype(jnp.float32)
    odd = lax.axis_index("rep") % 2
    agg = jnp.concatenate(
        [jnp.where(odd == 0, sums[0], sums[1]), jnp.where(odd == 0, sums[1], sums[0])], axis=1
    )
    mixed = ((agg + scaled_ref[...].astype(jnp.float32)) * inv_root).astype(jnp.bfloat16)
    pre = jnp.dot(mixed, weight_ref[...], preferred_element_type=jnp.float32) + bias_ref[...]
    square = pre * pre
    bent = jnp.tanh(GELU_C * (pre + 0.044715 * (square * pre)))
    half = 0.5 * (1.0 + bent)
    out_ref[...] = (pre * half).astype(jnp.bfloat16)
    inner = GELU_C * (1.0 + (3 * 0.044715) * square)
    slope = cotangent_ref[...].astype(jnp.float32) * (
        half + 0.5 * pre * ((1.0 - bent) * (1.0 + bent)) * inner
    )
    weight_term = lax.dot_general(
        mixed, slope.astype(jnp.bfloat16), (((0,), (0,)), ((), ())),
        preferred_element_type=jnp.float32,
    )
    bias_term = jnp.sum(slope, axis=0, keepdims=True)
    kept = width // 2
    top, bottom = weight_term[:kept], weight_term[kept:]
    core = lax.axis_index("dom") % 2
    keep_ref[:kept, :] = jnp.where(core == 0, top, bottom)
    send_ref[:kept, :] = jnp.where(core == 0, bottom, top)
    extra = jnp.broadcast_to(bias_term, (keep_ref.shape[0] - kept, width))
    keep_ref[kept:, :] = extra
    send_ref[kept:, :] = extra


def finish_kernel(mine_ref, other_ref, outcome_ref, weight_ref, bias_ref, out_ref):
    kept = weight_ref.shape[0] // 2
    first = lax.axis_index("dom") % 2 == 0
    mine = mine_ref[...].astype(jnp.float32)
    other = other_ref[...].astype(jnp.float32)
    weight_ref[:kept, :] = jnp.where(first, mine[:kept], other[:kept])
    weight_ref[kept:, :] = jnp.where(first, other[:kept], mine[:kept])
    bias_ref[...] = mine[kept : kept + 1]
    out_ref[...] = outcome_ref[...]


def xor_pairs(size, mask):
    return [(at, at ^ mask) for at in range(size)]


def exchange_sum(value, axis, masks):
    size = lax.axis_size(axis)
    while masks:
        now, masks = masks[:2], masks[2:]
        first = lax.ppermute(value, axis, xor_pairs(size, now[0]))
        if len(now) == 1:
            total = value.astype(jnp.float32) + first.astype(jnp.float32)
        else:
            second = lax.ppermute(value, axis, xor_pairs(size, now[1]))
            third = lax.ppermute(value, axis, xor_pairs(size, now[0] ^ now[1]))
            total = (value.astype(jnp.float32) + first.astype(jnp.float32)) + (
                second.astype(jnp.float32) + third.astype(jnp.float32)
            )
        value = total.astype(value.dtype)
    return value


def bits_of(size):
    return [1 << at for at in range(size.bit_length() - 1)]


def on_device(features, degree, tile_row, tile_col, tile_count, tile_live, weight, bias, cotangent):
    row_count, width = features.shape
    dom_size, rep_size = lax.axis_size("dom"), lax.axis_size("rep")
    sections, slots, block = tile_count.shape[1], tile_count.shape[2], tile_count.shape[3]
    block_count = row_count * rep_size // block
    degree_row = degree.reshape(1, row_count)
    bf16, f32 = jnp.bfloat16, jnp.float32
    half = jax.ShapeDtypeStruct((row_count, width // 2), bf16)

    outgoing = local_call(
        lambda *refs: scale_kernel(sections, *refs), "scale",
        (features, degree_row), [HBM] * 2, (half, half), (features, degree_row),
        [pltpu.SemaphoreType.DMA((2,))], 58,
    )
    arrived = []
    for flip, part in enumerate(outgoing):
        moves = []
        for dom in range(dom_size):
            plane = dom // sections
            for rep in range(rep_size):
                target = chip_of(plane, plane ^ flip, rep, rep_size) * sections + dom % sections
                moves.append((dom * rep_size + rep, target * rep_size + (plane ^ flip)))
        arrived.append(lax.ppermute(part, ("dom", "rep"), moves))

    tiles, scaled, inv_root, bias_row = local_call(
        lambda *refs: prepare_kernel(block_count, *refs), "prepare",
        (tile_count, tile_row, tile_col, features, degree_row, bias.reshape(1, width)),
        [VMEM, SMEM, SMEM, VMEM, VMEM, VMEM],
        (
            jax.ShapeDtypeStruct((sections * slots * block + CODE_ROWS, block), bf16),
            jax.ShapeDtypeStruct((row_count, width), bf16),
            jax.ShapeDtypeStruct((row_count, width // 2), f32),
            jax.ShapeDtypeStruct((1, width), f32),
        ),
    )
    their_tiles = lax.ppermute(tiles, "rep", xor_pairs(rep_size, 1))

    pieces = [None] * dom_size
    pieces[0] = local_call(
        join_kernel, "join", arrived, [VMEM] * 2,
        jax.ShapeDtypeStruct((2 * row_count, width // 2), bf16),
    )
    for mask in range(2, dom_size, 2):
        pieces[mask] = lax.ppermute(pieces[0], "dom", xor_pairs(dom_size, mask))
    for mask in range(0, dom_size, 2):
        pieces[mask + 1] = lax.ppermute(pieces[mask], "dom", xor_pairs(dom_size, 1))

    partials = local_call(
        lambda *refs: aggregate_kernel(dom_size, rep_size, sections, slots, *refs), "aggregate",
        (tiles, their_tiles, *pieces), [VMEM] * (2 + dom_size),
        (half,) * rep_size,
        (
            jax.ShapeDtypeStruct((dom_size * 2 * row_count // block, block, width // 2), bf16),
            jax.ShapeDtypeStruct((block_count, block, width // 2), f32),
        ),
    )

    parts = [partials[0]]
    for mask in range(1, rep_size):
        parts.append(lax.ppermute(partials[mask], "rep", xor_pairs(rep_size, mask)))

    share = jax.ShapeDtypeStruct((width // 2 + 16, width), f32)
    outcome, keep, send = local_call(
        lambda *refs: dense_kernel(rep_size, *refs), "dense",
        (*parts, scaled, inv_root, weight, bias_row, cotangent),
        [VMEM] * (rep_size + 5),
        (jax.ShapeDtypeStruct((row_count, width), bf16), share, share),
    )

    swap = xor_pairs(dom_size, 1)
    mine = (keep + lax.ppermute(send, "dom", swap)).astype(bf16)
    mine = exchange_sum(mine, "dom", bits_of(dom_size)[1:])
    mine = exchange_sum(mine, "rep", bits_of(rep_size))
    other = lax.ppermute(mine, "dom", swap)
    weight_grad, bias_grad, outcome = local_call(
        finish_kernel, "finish", (mine, other, outcome), [VMEM] * 3,
        (
            jax.ShapeDtypeStruct((width, width), f32),
            jax.ShapeDtypeStruct((1, width), f32),
            jax.ShapeDtypeStruct((row_count, width), bf16),
        ),
    )
    return (outcome, weight_grad, bias_grad.reshape(width))


def solution(mesh):
    return jax.shard_map(
        on_device,
        mesh=mesh,
        in_specs=(
            P(("dom", "rep"), None),
            P(("dom", "rep")),
            P("dom", "rep", None),
            P("dom", "rep", None),
            P("dom", "rep", None, None, None),
            P("dom", "rep"),
            P(),
            P(),
            P(("dom", "rep"), None),
        ),
        out_specs=(P(("dom", "rep"), None), P(), P()),
        check_vma=False,
    )
```

```python
import math

import jax
import jax.numpy as jnp
from jax import lax
from jax.experimental import pallas as pl
from jax.experimental.pallas import tpu as pltpu
from jax.sharding import PartitionSpec as P

VMEM = pl.BlockSpec(memory_space=pltpu.VMEM)
SMEM = pl.BlockSpec(memory_space=pltpu.SMEM)
HBM = pl.BlockSpec(memory_space=pltpu.MemorySpace.HBM)
CODE_ROWS = 16
GELU_C = 0.7978845608028654


ASIDE = ((3, 1, 2, 0), (1, 3, 2, 0), (0, 1, 3, 2), (0, 2, 1, 3))
ASIDE_BITS = sum(
    to << (2 * (4 * plane + rep)) for plane, row in enumerate(ASIDE) for rep, to in enumerate(row)
)


def chip_of(source, plane, rep, rep_size):
    if rep_size != 4:
        return source ^ rep
    if isinstance(plane, int):
        return source ^ ASIDE[plane][rep]
    bits = jnp.int32(ASIDE_BITS - (1 << 32) if ASIDE_BITS >> 31 else ASIDE_BITS)
    return source ^ (lax.shift_right_logical(bits, 2 * (4 * plane + rep)) & 3)


def local_call(kernel, name, inputs, in_specs, out_shape, scratch=(), small=(), spare=4):
    size = sum(
        math.prod(each.shape) * each.dtype.itemsize
        for each in (*inputs, *jax.tree.leaves(out_shape), *scratch)
    )
    return pl.pallas_call(
        kernel,
        out_shape=out_shape,
        in_specs=in_specs,
        out_specs=jax.tree.map(lambda each: VMEM, out_shape),
        scratch_shapes=[pltpu.VMEM(each.shape, each.dtype) for each in scratch] + list(small),
        compiler_params=pltpu.CompilerParams(vmem_limit_bytes=size + spare * 1024 * 1024),
        name=name,
    )(*inputs)


def column_of(row, width):
    return jnp.transpose(jnp.broadcast_to(row, (width, row.shape[1])))


def scale_kernel(sections, features_hbm, degree_hbm, *refs):
    out_refs, (features_ref, degree_ref, sems) = refs[:2], refs[2:]
    copies = [
        pltpu.make_async_copy(degree_hbm, degree_ref, sems.at[0]),
        pltpu.make_async_copy(features_hbm, features_ref, sems.at[1]),
    ]
    for copy in copies:
        copy.start()
    copies[0].wait()
    width = features_ref.shape[1] // 2
    inv_root = column_of(lax.rsqrt(degree_ref[...].astype(jnp.float32)), width)
    copies[1].wait()
    halves = []
    for half in range(2):
        part = features_ref[:, half * width : (half + 1) * width].astype(jnp.float32)
        halves.append((part * inv_root).astype(jnp.bfloat16))
    odd = (lax.axis_index("dom") // sections) % 2
    for out_ref, first, second in zip(out_refs, halves, halves[::-1]):
        out_ref[...] = jnp.where(odd == 0, first, second)


def prepare_kernel(
    block_count, count_ref, row_ref, col_ref, features_ref, degree_ref, bias_ref,
    tiles_ref, scaled_ref, inv_ref, bias_out_ref,
):
    _, sections, slots, block, _ = count_ref.shape
    for at in range(sections * slots):
        tile = count_ref[0, at // slots, at % slots].astype(jnp.float32)
        tiles_ref[at * block : (at + 1) * block, :] = tile.astype(jnp.bfloat16)
    lane = lax.broadcasted_iota(jnp.int32, (CODE_ROWS, block), 1)

    def code_step(at, codes):
        section, slot = at // slots, at % slots
        code = row_ref[0, section, slot] * block_count + col_ref[0, section, slot]
        return jnp.where(lane == at, code, codes)

    codes = lax.fori_loop(0, sections * slots, code_step, jnp.zeros_like(lane))
    tiles_ref[sections * slots * block :, :] = codes.astype(jnp.float32).astype(jnp.bfloat16)
    width = inv_ref.shape[1]
    inv_root = column_of(lax.rsqrt(degree_ref[...].astype(jnp.float32)), width)
    inv_ref[...] = inv_root
    for at in range(0, features_ref.shape[1], width):
        part = features_ref[:, at : at + width].astype(jnp.float32)
        scaled_ref[:, at : at + width] = (part * inv_root).astype(jnp.bfloat16)
    bias_out_ref[...] = bias_ref[...]


def join_kernel(first_ref, second_ref, out_ref):
    rows = first_ref.shape[0]
    out_ref[:rows, :] = first_ref[...]
    out_ref[rows:, :] = second_ref[...]


def aggregate_kernel(dom_size, rep_size, sections, slots, *refs):
    tile_refs, refs = refs[:2], refs[2:]
    piece_refs, refs = refs[:dom_size], refs[dom_size:]
    out_refs, (held, acc) = refs[:rep_size], refs[rep_size:]
    block = tile_refs[0].shape[1]
    tile_rows = sections * slots * block
    block_count = acc.shape[0]
    per_piece = piece_refs[0].shape[0] // block
    per_slice = per_piece // 2
    code_rows = [tile_ref[tile_rows:, :].astype(jnp.float32) for tile_ref in tile_refs]
    lane = lax.broadcasted_iota(jnp.int32, code_rows[0].shape, 1)
    dom, rep = lax.axis_index("dom"), lax.axis_index("rep")

    def code_of(which, at):
        return jnp.max(jnp.where(lane == at, code_rows[which], 0.0)).astype(jnp.int32)

    def add_slot(which, at, code):
        row, col = code // block_count, code % block_count
        chip = chip_of(rep ^ (which * (rep_size - 1)), rep, col // per_slice, rep_size)
        mask = (chip * sections + at // slots) ^ dom
        rows = held[mask * per_piece + which * per_slice + col % per_slice]
        tile = tile_refs[which][pl.ds(at * block, block), :]
        acc[row] += jnp.dot(tile, rows, preferred_element_type=jnp.float32)

    def both_step(at, carry):
        for which in range(2):
            add_slot(which, at, code_of(which, at))
        return carry

    few = sections * slots <= 8
    order = [(which, at) for which in range(2) for at in range(sections * slots)]
    codes = [code_of(*each) for each in order] if few else None
    for mask, piece_ref in enumerate(piece_refs):
        for at in range(per_piece):
            held[mask * per_piece + at] = piece_ref[at * block : (at + 1) * block, :]
    acc[...] = jnp.zeros_like(acc)
    if few:
        for (which, at), code in zip(order, codes):
            add_slot(which, at, code)
    else:
        lax.fori_loop(0, sections * slots, both_step, 0)

    for mask, out_ref in enumerate(out_refs):
        for at in range(per_slice):
            part = acc[(rep ^ mask) * per_slice + at]
            out_ref[at * block : (at + 1) * block, :] = part.astype(jnp.bfloat16)


def dense_kernel(rep_size, *refs):
    part_refs, refs = refs[:rep_size], refs[rep_size:]
    scaled_ref, inv_ref, weight_ref, bias_ref, cotangent_ref, out_ref, keep_ref, send_ref = refs
    width = scaled_ref.shape[1]
    inv_root = jnp.concatenate([inv_ref[...]] * 2, axis=1)
    sums = [0.0, 0.0]
    for mask, part_ref in enumerate(part_refs):
        sums[mask % 2] += part_ref[...].astype(jnp.float32)
    odd = lax.axis_index("rep") % 2
    agg = jnp.concatenate(
        [jnp.where(odd == 0, sums[0], sums[1]), jnp.where(odd == 0, sums[1], sums[0])], axis=1
    )
    mixed = ((agg + scaled_ref[...].astype(jnp.float32)) * inv_root).astype(jnp.bfloat16)
    pre = jnp.dot(mixed, weight_ref[...], preferred_element_type=jnp.float32) + bias_ref[...]
    square = pre * pre
    bent = jnp.tanh(GELU_C * (pre + 0.044715 * (square * pre)))
    half = 0.5 * (1.0 + bent)
    out_ref[...] = (pre * half).astype(jnp.bfloat16)
    inner = GELU_C * (1.0 + (3 * 0.044715) * square)
    slope = cotangent_ref[...].astype(jnp.float32) * (
        half + 0.5 * pre * ((1.0 - bent) * (1.0 + bent)) * inner
    )
    weight_term = lax.dot_general(
        mixed, slope.astype(jnp.bfloat16), (((0,), (0,)), ((), ())),
        preferred_element_type=jnp.float32,
    )
    bias_term = jnp.sum(slope, axis=0, keepdims=True)
    kept = width // 2
    top, bottom = weight_term[:kept], weight_term[kept:]
    core = lax.axis_index("dom") % 2
    keep_ref[:kept, :] = jnp.where(core == 0, top, bottom)
    send_ref[:kept, :] = jnp.where(core == 0, bottom, top)
    extra = jnp.broadcast_to(bias_term, (keep_ref.shape[0] - kept, width))
    keep_ref[kept:, :] = extra
    send_ref[kept:, :] = extra


def finish_kernel(mine_ref, other_ref, outcome_ref, weight_ref, bias_ref, out_ref):
    kept = weight_ref.shape[0] // 2
    first = lax.axis_index("dom") % 2 == 0
    mine = mine_ref[...].astype(jnp.float32)
    other = other_ref[...].astype(jnp.float32)
    weight_ref[:kept, :] = jnp.where(first, mine[:kept], other[:kept])
    weight_ref[kept:, :] = jnp.where(first, other[:kept], mine[:kept])
    bias_ref[...] = mine[kept : kept + 1]
    out_ref[...] = outcome_ref[...]


def xor_pairs(size, mask):
    return [(at, at ^ mask) for at in range(size)]


def exchange_sum(value, axis, masks):
    size = lax.axis_size(axis)
    while masks:
        now, masks = masks[:2], masks[2:]
        first = lax.ppermute(value, axis, xor_pairs(size, now[0]))
        if len(now) == 1:
            total = value.astype(jnp.float32) + first.astype(jnp.float32)
        else:
            second = lax.ppermute(value, axis, xor_pairs(size, now[1]))
            third = lax.ppermute(value, axis, xor_pairs(size, now[0] ^ now[1]))
            total = (value.astype(jnp.float32) + first.astype(jnp.float32)) + (
                second.astype(jnp.float32) + third.astype(jnp.float32)
            )
        value = total.astype(value.dtype)
    return value


def bits_of(size):
    return [1 << at for at in range(size.bit_length() - 1)]


def on_device(features, degree, tile_row, tile_col, tile_count, tile_live, weight, bias, cotangent):
    row_count, width = features.shape
    dom_size, rep_size = lax.axis_size("dom"), lax.axis_size("rep")
    sections, slots, block = tile_count.shape[1], tile_count.shape[2], tile_count.shape[3]
    block_count = row_count * rep_size // block
    degree_row = degree.reshape(1, row_count)
    bf16, f32 = jnp.bfloat16, jnp.float32
    half = jax.ShapeDtypeStruct((row_count, width // 2), bf16)

    outgoing = local_call(
        lambda *refs: scale_kernel(sections, *refs), "scale",
        (features, degree_row), [HBM] * 2, (half, half), (features, degree_row),
        [pltpu.SemaphoreType.DMA((2,))], 58,
    )
    arrived = []
    for flip, part in enumerate(outgoing):
        moves = []
        for dom in range(dom_size):
            plane = dom // sections
            for rep in range(rep_size):
                target = chip_of(plane, plane ^ (flip * (rep_size - 1)), rep, rep_size) * sections + dom % sections
                moves.append((dom * rep_size + rep, target * rep_size + (plane ^ (flip * (rep_size - 1)))))
        arrived.append(lax.ppermute(part, ("dom", "rep"), moves))

    tiles, scaled, inv_root, bias_row = local_call(
        lambda *refs: prepare_kernel(block_count, *refs), "prepare",
        (tile_count, tile_row, tile_col, features, degree_row, bias.reshape(1, width)),
        [VMEM, SMEM, SMEM, VMEM, VMEM, VMEM],
        (
            jax.ShapeDtypeStruct((sections * slots * block + CODE_ROWS, block), bf16),
            jax.ShapeDtypeStruct((row_count, width), bf16),
            jax.ShapeDtypeStruct((row_count, width // 2), f32),
            jax.ShapeDtypeStruct((1, width), f32),
        ),
    )
    their_tiles = lax.ppermute(tiles, "rep", xor_pairs(rep_size, rep_size - 1))

    pieces = [None] * dom_size
    pieces[0] = local_call(
        join_kernel, "join", arrived, [VMEM] * 2,
        jax.ShapeDtypeStruct((2 * row_count, width // 2), bf16),
    )
    for mask in range(2, dom_size, 2):
        pieces[mask] = lax.ppermute(pieces[0], "dom", xor_pairs(dom_size, mask))
    for mask in range(0, dom_size, 2):
        pieces[mask + 1] = lax.ppermute(pieces[mask], "dom", xor_pairs(dom_size, 1))

    partials = local_call(
        lambda *refs: aggregate_kernel(dom_size, rep_size, sections, slots, *refs), "aggregate",
        (tiles, their_tiles, *pieces), [VMEM] * (2 + dom_size),
        (half,) * rep_size,
        (
            jax.ShapeDtypeStruct((dom_size * 2 * row_count // block, block, width // 2), bf16),
            jax.ShapeDtypeStruct((block_count, block, width // 2), f32),
        ),
    )

    parts = [partials[0]]
    for mask in range(1, rep_size):
        parts.append(lax.ppermute(partials[mask], "rep", xor_pairs(rep_size, mask)))

    share = jax.ShapeDtypeStruct((width // 2 + 16, width), f32)
    outcome, keep, send = local_call(
        lambda *refs: dense_kernel(rep_size, *refs), "dense",
        (*parts, scaled, inv_root, weight, bias_row, cotangent),
        [VMEM] * (rep_size + 5),
        (jax.ShapeDtypeStruct((row_count, width), bf16), share, share),
    )

    swap = xor_pairs(dom_size, 1)
    mine = (keep + lax.ppermute(send, "dom", swap)).astype(bf16)
    mine = exchange_sum(mine, "dom", bits_of(dom_size)[1:])
    mine = exchange_sum(mine, "rep", bits_of(rep_size))
    other = lax.ppermute(mine, "dom", swap)
    weight_grad, bias_grad, outcome = local_call(
        finish_kernel, "finish", (mine, other, outcome), [VMEM] * 3,
        (
            jax.ShapeDtypeStruct((width, width), f32),
            jax.ShapeDtypeStruct((1, width), f32),
            jax.ShapeDtypeStruct((row_count, width), bf16),
        ),
    )
    return (outcome, weight_grad, bias_grad.reshape(width))


def solution(mesh):
    return jax.shard_map(
        on_device,
        mesh=mesh,
        in_specs=(
            P(("dom", "rep"), None),
            P(("dom", "rep")),
            P("dom", "rep", None),
            P("dom", "rep", None),
            P("dom", "rep", None, None, None),
            P("dom", "rep"),
            P(),
            P(),
            P(("dom", "rep"), None),
        ),
        out_specs=(P(("dom", "rep"), None), P(), P()),
        check_vma=False,
    )
```

```python
import math

import jax
import jax.numpy as jnp
from jax import lax
from jax.experimental import pallas as pl
from jax.experimental.pallas import tpu as pltpu
from jax.sharding import PartitionSpec as P

VMEM = pl.BlockSpec(memory_space=pltpu.VMEM)
SMEM = pl.BlockSpec(memory_space=pltpu.SMEM)
HBM = pl.BlockSpec(memory_space=pltpu.MemorySpace.HBM)
CODE_ROWS = 16
GELU_C = 0.7978845608028654


ASIDE = ((3, 2, 1, 0), (1, 3, 2, 0), (0, 1, 3, 2), (0, 1, 2, 3))
ASIDE_BITS = sum(
    to << (2 * (4 * plane + rep)) for plane, row in enumerate(ASIDE) for rep, to in enumerate(row)
)


def chip_of(source, plane, rep, rep_size):
    if rep_size != 4:
        return source ^ rep
    if isinstance(plane, int):
        return source ^ ASIDE[plane][rep]
    bits = jnp.int32(ASIDE_BITS - (1 << 32) if ASIDE_BITS >> 31 else ASIDE_BITS)
    return source ^ (lax.shift_right_logical(bits, 2 * (4 * plane + rep)) & 3)


def local_call(kernel, name, inputs, in_specs, out_shape, scratch=(), small=(), spare=4):
    size = sum(
        math.prod(each.shape) * each.dtype.itemsize
        for each in (*inputs, *jax.tree.leaves(out_shape), *scratch)
    )
    return pl.pallas_call(
        kernel,
        out_shape=out_shape,
        in_specs=in_specs,
        out_specs=jax.tree.map(lambda each: VMEM, out_shape),
        scratch_shapes=[pltpu.VMEM(each.shape, each.dtype) for each in scratch] + list(small),
        compiler_params=pltpu.CompilerParams(vmem_limit_bytes=size + spare * 1024 * 1024),
        name=name,
    )(*inputs)


def column_of(row, width):
    return jnp.transpose(jnp.broadcast_to(row, (width, row.shape[1])))


def scale_kernel(sections, features_hbm, degree_hbm, *refs):
    out_refs, (features_ref, degree_ref, sems) = refs[:2], refs[2:]
    copies = [
        pltpu.make_async_copy(degree_hbm, degree_ref, sems.at[0]),
        pltpu.make_async_copy(features_hbm, features_ref, sems.at[1]),
    ]
    for copy in copies:
        copy.start()
    copies[0].wait()
    width = features_ref.shape[1] // 2
    inv_root = column_of(lax.rsqrt(degree_ref[...].astype(jnp.float32)), width)
    copies[1].wait()
    halves = []
    for half in range(2):
        part = features_ref[:, half * width : (half + 1) * width].astype(jnp.float32)
        halves.append((part * inv_root).astype(jnp.bfloat16))
    odd = (lax.axis_index("dom") // sections) % 2
    for out_ref, first, second in zip(out_refs, halves, halves[::-1]):
        out_ref[...] = jnp.where(odd == 0, first, second)


def prepare_kernel(
    block_count, count_ref, row_ref, col_ref, features_ref, degree_ref, bias_ref,
    tiles_ref, scaled_ref, inv_ref, bias_out_ref,
):
    _, sections, slots, block, _ = count_ref.shape
    for at in range(sections * slots):
        tile = count_ref[0, at // slots, at % slots].astype(jnp.float32)
        tiles_ref[at * block : (at + 1) * block, :] = tile.astype(jnp.bfloat16)
    lane = lax.broadcasted_iota(jnp.int32, (CODE_ROWS, block), 1)

    def code_step(at, codes):
        section, slot = at // slots, at % slots
        code = row_ref[0, section, slot] * block_count + col_ref[0, section, slot]
        return jnp.where(lane == at, code, codes)

    codes = lax.fori_loop(0, sections * slots, code_step, jnp.zeros_like(lane))
    tiles_ref[sections * slots * block :, :] = codes.astype(jnp.float32).astype(jnp.bfloat16)
    width = inv_ref.shape[1]
    inv_root = column_of(lax.rsqrt(degree_ref[...].astype(jnp.float32)), width)
    inv_ref[...] = inv_root
    for at in range(0, features_ref.shape[1], width):
        part = features_ref[:, at : at + width].astype(jnp.float32)
        scaled_ref[:, at : at + width] = (part * inv_root).astype(jnp.bfloat16)
    bias_out_ref[...] = bias_ref[...]


def join_kernel(first_ref, second_ref, out_ref):
    rows = first_ref.shape[0]
    out_ref[:rows, :] = first_ref[...]
    out_ref[rows:, :] = second_ref[...]


def aggregate_kernel(dom_size, rep_size, sections, slots, *refs):
    tile_refs, refs = refs[:2], refs[2:]
    piece_refs, refs = refs[:dom_size], refs[dom_size:]
    out_refs, (held, acc) = refs[:rep_size], refs[rep_size:]
    block = tile_refs[0].shape[1]
    tile_rows = sections * slots * block
    block_count = acc.shape[0]
    per_piece = piece_refs[0].shape[0] // block
    per_slice = per_piece // 2
    code_rows = [tile_ref[tile_rows:, :].astype(jnp.float32) for tile_ref in tile_refs]
    lane = lax.broadcasted_iota(jnp.int32, code_rows[0].shape, 1)
    dom, rep = lax.axis_index("dom"), lax.axis_index("rep")

    def code_of(which, at):
        return jnp.max(jnp.where(lane == at, code_rows[which], 0.0)).astype(jnp.int32)

    def add_slot(which, at, code):
        row, col = code // block_count, code % block_count
        chip = chip_of(rep ^ (which * (rep_size - 1)), rep, col // per_slice, rep_size)
        mask = (chip * sections + at // slots) ^ dom
        rows = held[mask * per_piece + which * per_slice + col % per_slice]
        tile = tile_refs[which][pl.ds(at * block, block), :]
        acc[row] += jnp.dot(tile, rows, preferred_element_type=jnp.float32)

    def both_step(at, carry):
        for which in range(2):
            add_slot(which, at, code_of(which, at))
        return carry

    few = sections * slots <= 8
    order = [(which, at) for which in range(2) for at in range(sections * slots)]
    codes = [code_of(*each) for each in order] if few else None
    for mask, piece_ref in enumerate(piece_refs):
        for at in range(per_piece):
            held[mask * per_piece + at] = piece_ref[at * block : (at + 1) * block, :]
    acc[...] = jnp.zeros_like(acc)
    if few:
        for (which, at), code in zip(order, codes):
            add_slot(which, at, code)
    else:
        lax.fori_loop(0, sections * slots, both_step, 0)

    for mask, out_ref in enumerate(out_refs):
        for at in range(per_slice):
            part = acc[(rep ^ mask) * per_slice + at]
            out_ref[at * block : (at + 1) * block, :] = part.astype(jnp.bfloat16)


def dense_kernel(rep_size, *refs):
    part_refs, refs = refs[:rep_size], refs[rep_size:]
    scaled_ref, inv_ref, weight_ref, bias_ref, cotangent_ref, out_ref, keep_ref, send_ref = refs
    width = scaled_ref.shape[1]
    inv_root = jnp.concatenate([inv_ref[...]] * 2, axis=1)
    sums = [0.0, 0.0]
    for mask, part_ref in enumerate(part_refs):
        sums[mask % 2] += part_ref[...].astype(jnp.float32)
    odd = lax.axis_index("rep") % 2
    agg = jnp.concatenate(
        [jnp.where(odd == 0, sums[0], sums[1]), jnp.where(odd == 0, sums[1], sums[0])], axis=1
    )
    mixed = ((agg + scaled_ref[...].astype(jnp.float32)) * inv_root).astype(jnp.bfloat16)
    pre = jnp.dot(mixed, weight_ref[...], preferred_element_type=jnp.float32) + bias_ref[...]
    square = pre * pre
    bent = jnp.tanh(GELU_C * (pre + 0.044715 * (square * pre)))
    half = 0.5 * (1.0 + bent)
    out_ref[...] = (pre * half).astype(jnp.bfloat16)
    inner = GELU_C * (1.0 + (3 * 0.044715) * square)
    slope = cotangent_ref[...].astype(jnp.float32) * (
        half + 0.5 * pre * ((1.0 - bent) * (1.0 + bent)) * inner
    )
    weight_term = lax.dot_general(
        mixed, slope.astype(jnp.bfloat16), (((0,), (0,)), ((), ())),
        preferred_element_type=jnp.float32,
    )
    bias_term = jnp.sum(slope, axis=0, keepdims=True)
    kept = width // 2
    top, bottom = weight_term[:kept], weight_term[kept:]
    core = lax.axis_index("dom") % 2
    keep_ref[:kept, :] = jnp.where(core == 0, top, bottom)
    send_ref[:kept, :] = jnp.where(core == 0, bottom, top).astype(jnp.bfloat16)
    extra = jnp.broadcast_to(bias_term, (keep_ref.shape[0] - kept, width))
    keep_ref[kept:, :] = extra
    send_ref[kept:, :] = extra.astype(jnp.bfloat16)


def finish_kernel(mine_ref, other_ref, outcome_ref, weight_ref, bias_ref, out_ref):
    kept = weight_ref.shape[0] // 2
    first = lax.axis_index("dom") % 2 == 0
    mine = mine_ref[...].astype(jnp.float32)
    other = other_ref[...].astype(jnp.float32)
    weight_ref[:kept, :] = jnp.where(first, mine[:kept], other[:kept])
    weight_ref[kept:, :] = jnp.where(first, other[:kept], mine[:kept])
    bias_ref[...] = mine[kept : kept + 1]
    out_ref[...] = outcome_ref[...]


def xor_pairs(size, mask):
    return [(at, at ^ mask) for at in range(size)]


def exchange_sum(value, axis, masks):
    size = lax.axis_size(axis)
    while masks:
        now, masks = masks[:2], masks[2:]
        first = lax.ppermute(value, axis, xor_pairs(size, now[0]))
        if len(now) == 1:
            total = value.astype(jnp.float32) + first.astype(jnp.float32)
        else:
            second = lax.ppermute(value, axis, xor_pairs(size, now[1]))
            third = lax.ppermute(value, axis, xor_pairs(size, now[0] ^ now[1]))
            total = (value.astype(jnp.float32) + first.astype(jnp.float32)) + (
                second.astype(jnp.float32) + third.astype(jnp.float32)
            )
        value = total.astype(value.dtype)
    return value


def bits_of(size):
    return [1 << at for at in range(size.bit_length() - 1)]


def on_device(features, degree, tile_row, tile_col, tile_count, tile_live, weight, bias, cotangent):
    row_count, width = features.shape
    dom_size, rep_size = lax.axis_size("dom"), lax.axis_size("rep")
    sections, slots, block = tile_count.shape[1], tile_count.shape[2], tile_count.shape[3]
    block_count = row_count * rep_size // block
    degree_row = degree.reshape(1, row_count)
    bf16, f32 = jnp.bfloat16, jnp.float32
    half = jax.ShapeDtypeStruct((row_count, width // 2), bf16)

    outgoing = local_call(
        lambda *refs: scale_kernel(sections, *refs), "scale",
        (features, degree_row), [HBM] * 2, (half, half), (features, degree_row),
        [pltpu.SemaphoreType.DMA((2,))], 58,
    )
    arrived = []
    for flip, part in enumerate(outgoing):
        moves = []
        for dom in range(dom_size):
            plane = dom // sections
            for rep in range(rep_size):
                target = chip_of(plane, plane ^ (flip * (rep_size - 1)), rep, rep_size) * sections + dom % sections
                moves.append((dom * rep_size + rep, target * rep_size + (plane ^ (flip * (rep_size - 1)))))
        arrived.append(lax.ppermute(part, ("dom", "rep"), moves))

    tiles, scaled, inv_root, bias_row = local_call(
        lambda *refs: prepare_kernel(block_count, *refs), "prepare",
        (tile_count, tile_row, tile_col, features, degree_row, bias.reshape(1, width)),
        [VMEM, SMEM, SMEM, VMEM, VMEM, VMEM],
        (
            jax.ShapeDtypeStruct((sections * slots * block + CODE_ROWS, block), bf16),
            jax.ShapeDtypeStruct((row_count, width), bf16),
            jax.ShapeDtypeStruct((row_count, width // 2), f32),
            jax.ShapeDtypeStruct((1, width), f32),
        ),
    )
    their_tiles = lax.ppermute(tiles, "rep", xor_pairs(rep_size, rep_size - 1))

    pieces = [None] * dom_size
    pieces[0] = local_call(
        join_kernel, "join", arrived, [VMEM] * 2,
        jax.ShapeDtypeStruct((2 * row_count, width // 2), bf16),
    )
    for mask in range(2, dom_size, 2):
        pieces[mask] = lax.ppermute(pieces[0], "dom", xor_pairs(dom_size, mask))
    for mask in range(0, dom_size, 2):
        pieces[mask + 1] = lax.ppermute(pieces[mask], "dom", xor_pairs(dom_size, 1))

    partials = local_call(
        lambda *refs: aggregate_kernel(dom_size, rep_size, sections, slots, *refs), "aggregate",
        (tiles, their_tiles, *pieces), [VMEM] * (2 + dom_size),
        (half,) * rep_size,
        (
            jax.ShapeDtypeStruct((dom_size * 2 * row_count // block, block, width // 2), bf16),
            jax.ShapeDtypeStruct((block_count, block, width // 2), f32),
        ),
    )

    parts = [partials[0]]
    for mask in range(1, rep_size):
        parts.append(lax.ppermute(partials[mask], "rep", xor_pairs(rep_size, mask)))

    share = [jax.ShapeDtypeStruct((width // 2 + 16, width), each) for each in (f32, bf16)]
    outcome, keep, send = local_call(
        lambda *refs: dense_kernel(rep_size, *refs), "dense",
        (*parts, scaled, inv_root, weight, bias_row, cotangent),
        [VMEM] * (rep_size + 5),
        (jax.ShapeDtypeStruct((row_count, width), bf16), *share),
    )

    swap = xor_pairs(dom_size, 1)
    mine = (keep + lax.ppermute(send, "dom", swap).astype(f32)).astype(bf16)
    mine = exchange_sum(mine, "dom", bits_of(dom_size)[1:])
    mine = exchange_sum(mine, "rep", bits_of(rep_size))
    other = lax.ppermute(mine, "dom", swap)
    weight_grad, bias_grad, outcome = local_call(
        finish_kernel, "finish", (mine, other, outcome), [VMEM] * 3,
        (
            jax.ShapeDtypeStruct((width, width), f32),
            jax.ShapeDtypeStruct((1, width), f32),
            jax.ShapeDtypeStruct((row_count, width), bf16),
        ),
    )
    return (outcome, weight_grad, bias_grad.reshape(width))


def solution(mesh):
    return jax.shard_map(
        on_device,
        mesh=mesh,
        in_specs=(
            P(("dom", "rep"), None),
            P(("dom", "rep")),
            P("dom", "rep", None),
            P("dom", "rep", None),
            P("dom", "rep", None, None, None),
            P("dom", "rep"),
            P(),
            P(),
            P(("dom", "rep"), None),
        ),
        out_specs=(P(("dom", "rep"), None), P(), P()),
        check_vma=False,
    )
```

```python
import math

import jax
import jax.numpy as jnp
from jax import lax
from jax.experimental import pallas as pl
from jax.experimental.pallas import tpu as pltpu
from jax.sharding import PartitionSpec as P

VMEM = pl.BlockSpec(memory_space=pltpu.VMEM)
SMEM = pl.BlockSpec(memory_space=pltpu.SMEM)
HBM = pl.BlockSpec(memory_space=pltpu.MemorySpace.HBM)
CODE_ROWS = 16
GELU_C = 0.7978845608028654


ASIDE = ((3, 2, 1, 0), (1, 3, 2, 0), (0, 1, 3, 2), (0, 1, 2, 3))
ASIDE_BITS = sum(
    to << (2 * (4 * plane + rep)) for plane, row in enumerate(ASIDE) for rep, to in enumerate(row)
)


def chip_of(source, plane, rep, rep_size):
    if rep_size != 4:
        return source ^ rep
    if isinstance(plane, int):
        return source ^ ASIDE[plane][rep]
    bits = jnp.int32(ASIDE_BITS - (1 << 32) if ASIDE_BITS >> 31 else ASIDE_BITS)
    return source ^ (lax.shift_right_logical(bits, 2 * (4 * plane + rep)) & 3)


def local_call(kernel, name, inputs, in_specs, out_shape, scratch=(), small=(), spare=4):
    size = sum(
        math.prod(each.shape) * each.dtype.itemsize
        for each in (*inputs, *jax.tree.leaves(out_shape), *scratch)
    )
    return pl.pallas_call(
        kernel,
        out_shape=out_shape,
        in_specs=in_specs,
        out_specs=jax.tree.map(lambda each: VMEM, out_shape),
        scratch_shapes=[pltpu.VMEM(each.shape, each.dtype) for each in scratch] + list(small),
        compiler_params=pltpu.CompilerParams(vmem_limit_bytes=size + int(spare * 1024) * 1024),
        name=name,
    )(*inputs)


def column_of(row, width):
    return jnp.transpose(jnp.broadcast_to(row, (width, row.shape[1])))


def scale_kernel(sections, features_hbm, degree_hbm, *refs):
    out_refs, (features_ref, degree_ref, sems) = refs[:2], refs[2:]
    copies = [
        pltpu.make_async_copy(degree_hbm, degree_ref, sems.at[0]),
        pltpu.make_async_copy(features_hbm, features_ref, sems.at[1]),
    ]
    for copy in copies:
        copy.start()
    copies[0].wait()
    width = features_ref.shape[1] // 2
    inv_root = column_of(lax.rsqrt(degree_ref[...].astype(jnp.float32)), width)
    copies[1].wait()
    halves = []
    for half in range(2):
        part = features_ref[:, half * width : (half + 1) * width].astype(jnp.float32)
        halves.append((part * inv_root).astype(jnp.bfloat16))
    odd = (lax.axis_index("dom") // sections) % 2
    for out_ref, first, second in zip(out_refs, halves, halves[::-1]):
        out_ref[...] = jnp.where(odd == 0, first, second)


def prepare_kernel(
    block_count, count_ref, row_ref, col_ref, features_ref, degree_ref, bias_ref,
    tiles_ref, scaled_ref, inv_ref, bias_out_ref,
):
    _, sections, slots, block, _ = count_ref.shape
    for at in range(sections * slots):
        tile = count_ref[0, at // slots, at % slots].astype(jnp.float32)
        tiles_ref[at * block : (at + 1) * block, :] = tile.astype(jnp.bfloat16)
    lane = lax.broadcasted_iota(jnp.int32, (CODE_ROWS, block), 1)

    def code_step(at, codes):
        section, slot = at // slots, at % slots
        code = row_ref[0, section, slot] * block_count + col_ref[0, section, slot]
        return jnp.where(lane == at, code, codes)

    codes = lax.fori_loop(0, sections * slots, code_step, jnp.zeros_like(lane))
    tiles_ref[sections * slots * block :, :] = codes.astype(jnp.float32).astype(jnp.bfloat16)
    width = inv_ref.shape[1]
    inv_root = column_of(lax.rsqrt(degree_ref[...].astype(jnp.float32)), width)
    inv_ref[...] = inv_root
    for at in range(0, features_ref.shape[1], width):
        part = features_ref[:, at : at + width].astype(jnp.float32)
        scaled_ref[:, at : at + width] = (part * inv_root).astype(jnp.bfloat16)
    bias_out_ref[...] = bias_ref[...]


def join_kernel(first_ref, second_ref, out_ref):
    rows = first_ref.shape[0]
    out_ref[:rows, :] = first_ref[...]
    out_ref[rows:, :] = second_ref[...]


def aggregate_kernel(dom_size, rep_size, sections, slots, *refs):
    tile_refs, refs = refs[:2], refs[2:]
    piece_refs, refs = refs[:dom_size], refs[dom_size:]
    out_refs, (held, acc) = refs[:rep_size], refs[rep_size:]
    block = tile_refs[0].shape[1]
    tile_rows = sections * slots * block
    block_count = acc.shape[0]
    per_piece = piece_refs[0].shape[0] // block
    per_slice = per_piece // 2
    code_rows = [tile_ref[tile_rows:, :].astype(jnp.float32) for tile_ref in tile_refs]
    lane = lax.broadcasted_iota(jnp.int32, code_rows[0].shape, 1)
    dom, rep = lax.axis_index("dom"), lax.axis_index("rep")

    def code_of(which, at):
        return jnp.max(jnp.where(lane == at, code_rows[which], 0.0)).astype(jnp.int32)

    def add_slot(which, at, code):
        row, col = code // block_count, code % block_count
        chip = chip_of(rep ^ (which * (rep_size - 1)), rep, col // per_slice, rep_size)
        mask = (chip * sections + at // slots) ^ dom
        rows = held[mask * per_piece + which * per_slice + col % per_slice]
        tile = tile_refs[which][pl.ds(at * block, block), :]
        acc[row] += jnp.dot(tile, rows, preferred_element_type=jnp.float32)

    def both_step(at, carry):
        for which in range(2):
            add_slot(which, at, code_of(which, at))
        return carry

    few = sections * slots <= 8
    order = [(which, at) for which in range(2) for at in range(sections * slots)]
    codes = [code_of(*each) for each in order] if few else None
    for mask, piece_ref in enumerate(piece_refs):
        for at in range(per_piece):
            held[mask * per_piece + at] = piece_ref[at * block : (at + 1) * block, :]
    acc[...] = jnp.zeros_like(acc)
    if few:
        for (which, at), code in zip(order, codes):
            add_slot(which, at, code)
    else:
        lax.fori_loop(0, sections * slots, both_step, 0)

    for mask, out_ref in enumerate(out_refs):
        for at in range(per_slice):
            part = acc[(rep ^ mask) * per_slice + at]
            out_ref[at * block : (at + 1) * block, :] = part.astype(jnp.bfloat16)


def dense_kernel(rep_size, *refs):
    part_refs, refs = refs[:rep_size], refs[rep_size:]
    scaled_ref, inv_ref, weight_ref, bias_ref, cotangent_ref, out_ref, keep_ref, send_ref = refs
    width = scaled_ref.shape[1]
    inv_root = jnp.concatenate([inv_ref[...]] * 2, axis=1)
    sums = [0.0, 0.0]
    for mask, part_ref in enumerate(part_refs):
        sums[mask % 2] += part_ref[...].astype(jnp.float32)
    odd = lax.axis_index("rep") % 2
    agg = jnp.concatenate(
        [jnp.where(odd == 0, sums[0], sums[1]), jnp.where(odd == 0, sums[1], sums[0])], axis=1
    )
    mixed = ((agg + scaled_ref[...].astype(jnp.float32)) * inv_root).astype(jnp.bfloat16)
    pre = jnp.dot(mixed, weight_ref[...], preferred_element_type=jnp.float32) + bias_ref[...]
    square = pre * pre
    bent = jnp.tanh(GELU_C * (pre + 0.044715 * (square * pre)))
    half = 0.5 * (1.0 + bent)
    out_ref[...] = (pre * half).astype(jnp.bfloat16)
    inner = GELU_C * (1.0 + (3 * 0.044715) * square)
    slope = cotangent_ref[...].astype(jnp.float32) * (
        half + 0.5 * pre * ((1.0 - bent) * (1.0 + bent)) * inner
    )
    weight_term = lax.dot_general(
        mixed, slope.astype(jnp.bfloat16), (((0,), (0,)), ((), ())),
        preferred_element_type=jnp.float32,
    )
    bias_term = jnp.sum(slope, axis=0, keepdims=True)
    kept = width // 2
    top, bottom = weight_term[:kept], weight_term[kept:]
    core = lax.axis_index("dom") % 2
    keep_ref[:kept, :] = jnp.where(core == 0, top, bottom)
    send_ref[:kept, :] = jnp.where(core == 0, bottom, top).astype(jnp.bfloat16)
    extra = jnp.broadcast_to(bias_term, (keep_ref.shape[0] - kept, width))
    keep_ref[kept:, :] = extra
    send_ref[kept:, :] = extra.astype(jnp.bfloat16)


def finish_kernel(mine_ref, other_ref, outcome_ref, weight_ref, bias_ref, out_ref):
    kept = weight_ref.shape[0] // 2
    first = lax.axis_index("dom") % 2 == 0
    mine = mine_ref[...].astype(jnp.float32)
    other = other_ref[...].astype(jnp.float32)
    weight_ref[:kept, :] = jnp.where(first, mine[:kept], other[:kept])
    weight_ref[kept:, :] = jnp.where(first, other[:kept], mine[:kept])
    bias_ref[...] = mine[kept : kept + 1]
    out_ref[...] = outcome_ref[...]


def xor_pairs(size, mask):
    return [(at, at ^ mask) for at in range(size)]


def exchange_sum(value, axis, masks):
    size = lax.axis_size(axis)
    while masks:
        now, masks = masks[:2], masks[2:]
        first = lax.ppermute(value, axis, xor_pairs(size, now[0]))
        if len(now) == 1:
            total = value.astype(jnp.float32) + first.astype(jnp.float32)
        else:
            second = lax.ppermute(value, axis, xor_pairs(size, now[1]))
            third = lax.ppermute(value, axis, xor_pairs(size, now[0] ^ now[1]))
            total = (value.astype(jnp.float32) + first.astype(jnp.float32)) + (
                second.astype(jnp.float32) + third.astype(jnp.float32)
            )
        value = total.astype(value.dtype)
    return value


def bits_of(size):
    return [1 << at for at in range(size.bit_length() - 1)]


def on_device(features, degree, tile_row, tile_col, tile_count, tile_live, weight, bias, cotangent):
    row_count, width = features.shape
    dom_size, rep_size = lax.axis_size("dom"), lax.axis_size("rep")
    sections, slots, block = tile_count.shape[1], tile_count.shape[2], tile_count.shape[3]
    block_count = row_count * rep_size // block
    degree_row = degree.reshape(1, row_count)
    bf16, f32 = jnp.bfloat16, jnp.float32
    half = jax.ShapeDtypeStruct((row_count, width // 2), bf16)

    outgoing = local_call(
        lambda *refs: scale_kernel(sections, *refs), "scale",
        (features, degree_row), [HBM] * 2, (half, half), (features, degree_row),
        [pltpu.SemaphoreType.DMA((2,))], 53.375,
    )
    arrived = []
    for flip, part in enumerate(outgoing):
        moves = []
        for dom in range(dom_size):
            plane = dom // sections
            for rep in range(rep_size):
                target = chip_of(plane, plane ^ (flip * (rep_size - 1)), rep, rep_size) * sections + dom % sections
                moves.append((dom * rep_size + rep, target * rep_size + (plane ^ (flip * (rep_size - 1)))))
        arrived.append(lax.ppermute(part, ("dom", "rep"), moves))

    tiles, scaled, inv_root, bias_row = local_call(
        lambda *refs: prepare_kernel(block_count, *refs), "prepare",
        (tile_count, tile_row, tile_col, features, degree_row, bias.reshape(1, width)),
        [VMEM, SMEM, SMEM, VMEM, VMEM, VMEM],
        (
            jax.ShapeDtypeStruct((sections * slots * block + CODE_ROWS, block), bf16),
            jax.ShapeDtypeStruct((row_count, width), bf16),
            jax.ShapeDtypeStruct((row_count, width // 2), f32),
            jax.ShapeDtypeStruct((1, width), f32),
        ),
    )
    their_tiles = lax.ppermute(tiles, "rep", xor_pairs(rep_size, rep_size - 1))

    pieces = [None] * dom_size
    pieces[0] = local_call(
        join_kernel, "join", arrived, [VMEM] * 2,
        jax.ShapeDtypeStruct((2 * row_count, width // 2), bf16),
    )
    for mask in range(2, dom_size, 2):
        pieces[mask] = lax.ppermute(pieces[0], "dom", xor_pairs(dom_size, mask))
    for mask in range(0, dom_size, 2):
        pieces[mask + 1] = lax.ppermute(pieces[mask], "dom", xor_pairs(dom_size, 1))

    partials = local_call(
        lambda *refs: aggregate_kernel(dom_size, rep_size, sections, slots, *refs), "aggregate",
        (tiles, their_tiles, *pieces), [VMEM] * (2 + dom_size),
        (half,) * rep_size,
        (
            jax.ShapeDtypeStruct((dom_size * 2 * row_count // block, block, width // 2), bf16),
            jax.ShapeDtypeStruct((block_count, block, width // 2), f32),
        ),
    )

    parts = [partials[0]]
    for mask in range(1, rep_size):
        parts.append(lax.ppermute(partials[mask], "rep", xor_pairs(rep_size, mask)))

    share = [jax.ShapeDtypeStruct((width // 2 + 16, width), each) for each in (f32, bf16)]
    outcome, keep, send = local_call(
        lambda *refs: dense_kernel(rep_size, *refs), "dense",
        (*parts, scaled, inv_root, weight, bias_row, cotangent),
        [VMEM] * (rep_size + 5),
        (jax.ShapeDtypeStruct((row_count, width), bf16), *share),
    )

    swap = xor_pairs(dom_size, 1)
    mine = (keep + lax.ppermute(send, "dom", swap).astype(f32)).astype(bf16)
    mine = exchange_sum(mine, "dom", bits_of(dom_size)[1:])
    mine = exchange_sum(mine, "rep", bits_of(rep_size))
    other = lax.ppermute(mine, "dom", swap)
    weight_grad, bias_grad, outcome = local_call(
        finish_kernel, "finish", (mine, other, outcome), [VMEM] * 3,
        (
            jax.ShapeDtypeStruct((width, width), f32),
            jax.ShapeDtypeStruct((1, width), f32),
            jax.ShapeDtypeStruct((row_count, width), bf16),
        ),
    )
    return (outcome, weight_grad, bias_grad.reshape(width))


def solution(mesh):
    return jax.shard_map(
        on_device,
        mesh=mesh,
        in_specs=(
            P(("dom", "rep"), None),
            P(("dom", "rep")),
            P("dom", "rep", None),
            P("dom", "rep", None),
            P("dom", "rep", None, None, None),
            P("dom", "rep"),
            P(),
            P(),
            P(("dom", "rep"), None),
        ),
        out_specs=(P(("dom", "rep"), None), P(), P()),
        check_vma=False,
    )
```

```python
import math

import jax
import jax.numpy as jnp
from jax import lax
from jax.experimental import pallas as pl
from jax.experimental.pallas import tpu as pltpu
from jax.sharding import PartitionSpec as P

VMEM = pl.BlockSpec(memory_space=pltpu.VMEM)
SMEM = pl.BlockSpec(memory_space=pltpu.SMEM)
HBM = pl.BlockSpec(memory_space=pltpu.MemorySpace.HBM)
CODE_ROWS = 16
GELU_C = 0.7978845608028654


ASIDE = ((3, 2, 1, 0), (1, 2, 3, 0), (0, 3, 1, 2), (0, 1, 2, 3))
ASIDE_BITS = sum(
    to << (2 * (4 * plane + rep)) for plane, row in enumerate(ASIDE) for rep, to in enumerate(row)
)


def chip_of(source, plane, rep, rep_size):
    if rep_size != 4:
        return source ^ rep
    if isinstance(plane, int):
        return source ^ ASIDE[plane][rep]
    bits = jnp.int32(ASIDE_BITS - (1 << 32) if ASIDE_BITS >> 31 else ASIDE_BITS)
    return source ^ (lax.shift_right_logical(bits, 2 * (4 * plane + rep)) & 3)


def local_call(kernel, name, inputs, in_specs, out_shape, scratch=(), small=(), spare=4):
    size = sum(
        math.prod(each.shape) * each.dtype.itemsize
        for each in (*inputs, *jax.tree.leaves(out_shape), *scratch)
    )
    return pl.pallas_call(
        kernel,
        out_shape=out_shape,
        in_specs=in_specs,
        out_specs=jax.tree.map(lambda each: VMEM, out_shape),
        scratch_shapes=[pltpu.VMEM(each.shape, each.dtype) for each in scratch] + list(small),
        compiler_params=pltpu.CompilerParams(vmem_limit_bytes=size + int(spare * 1024) * 1024),
        name=name,
    )(*inputs)


def column_of(row, width):
    return jnp.transpose(jnp.broadcast_to(row, (width, row.shape[1])))


def scale_kernel(sections, features_hbm, degree_hbm, *refs):
    out_refs, (features_ref, degree_ref, sems) = refs[:2], refs[2:]
    copies = [
        pltpu.make_async_copy(degree_hbm, degree_ref, sems.at[0]),
        pltpu.make_async_copy(features_hbm, features_ref, sems.at[1]),
    ]
    for copy in copies:
        copy.start()
    copies[0].wait()
    width = features_ref.shape[1] // 2
    inv_root = column_of(lax.rsqrt(degree_ref[...].astype(jnp.float32)), width)
    copies[1].wait()
    halves = []
    for half in range(2):
        part = features_ref[:, half * width : (half + 1) * width].astype(jnp.float32)
        halves.append((part * inv_root).astype(jnp.bfloat16))
    odd = (lax.axis_index("dom") // sections) % 2
    for out_ref, first, second in zip(out_refs, halves, halves[::-1]):
        out_ref[...] = jnp.where(odd == 0, first, second)


def prepare_kernel(
    block_count, count_ref, row_ref, col_ref, features_ref, degree_ref, bias_ref,
    tiles_ref, scaled_ref, inv_ref, bias_out_ref,
):
    _, sections, slots, block, _ = count_ref.shape
    for at in range(sections * slots):
        tile = count_ref[0, at // slots, at % slots].astype(jnp.float32)
        tiles_ref[at * block : (at + 1) * block, :] = tile.astype(jnp.bfloat16)
    lane = lax.broadcasted_iota(jnp.int32, (CODE_ROWS, block), 1)

    def code_step(at, codes):
        section, slot = at // slots, at % slots
        code = row_ref[0, section, slot] * block_count + col_ref[0, section, slot]
        return jnp.where(lane == at, code, codes)

    codes = lax.fori_loop(0, sections * slots, code_step, jnp.zeros_like(lane))
    tiles_ref[sections * slots * block :, :] = codes.astype(jnp.float32).astype(jnp.bfloat16)
    width = inv_ref.shape[1]
    inv_root = column_of(lax.rsqrt(degree_ref[...].astype(jnp.float32)), width)
    inv_ref[...] = inv_root
    for at in range(0, features_ref.shape[1], width):
        part = features_ref[:, at : at + width].astype(jnp.float32)
        scaled_ref[:, at : at + width] = (part * inv_root).astype(jnp.bfloat16)
    bias_out_ref[...] = bias_ref[...]


def join_kernel(first_ref, second_ref, out_ref):
    rows = first_ref.shape[0]
    out_ref[:rows, :] = first_ref[...]
    out_ref[rows:, :] = second_ref[...]


def aggregate_kernel(dom_size, rep_size, sections, slots, *refs):
    tile_refs, refs = refs[:2], refs[2:]
    piece_refs, refs = refs[:dom_size], refs[dom_size:]
    out_refs, (held, acc) = refs[:rep_size], refs[rep_size:]
    block = tile_refs[0].shape[1]
    tile_rows = sections * slots * block
    block_count = acc.shape[0]
    per_piece = piece_refs[0].shape[0] // block
    per_slice = per_piece // 2
    code_rows = [tile_ref[tile_rows:, :].astype(jnp.float32) for tile_ref in tile_refs]
    lane = lax.broadcasted_iota(jnp.int32, code_rows[0].shape, 1)
    dom, rep = lax.axis_index("dom"), lax.axis_index("rep")

    def code_of(which, at):
        return jnp.max(jnp.where(lane == at, code_rows[which], 0.0)).astype(jnp.int32)

    def add_slot(which, at, code):
        row, col = code // block_count, code % block_count
        chip = chip_of(rep ^ (which * (rep_size - 1)), rep, col // per_slice, rep_size)
        mask = (chip * sections + at // slots) ^ dom
        rows = held[mask * per_piece + which * per_slice + col % per_slice]
        tile = tile_refs[which][pl.ds(at * block, block), :]
        acc[row] += jnp.dot(tile, rows, preferred_element_type=jnp.float32)

    def both_step(at, carry):
        for which in range(2):
            add_slot(which, at, code_of(which, at))
        return carry

    few = sections * slots <= 8
    order = [(which, at) for which in range(2) for at in range(sections * slots)]
    codes = [code_of(*each) for each in order] if few else None
    for mask, piece_ref in enumerate(piece_refs):
        for at in range(per_piece):
            held[mask * per_piece + at] = piece_ref[at * block : (at + 1) * block, :]
    acc[...] = jnp.zeros_like(acc)
    if few:
        for (which, at), code in zip(order, codes):
            add_slot(which, at, code)
    else:
        lax.fori_loop(0, sections * slots, both_step, 0)

    for mask, out_ref in enumerate(out_refs):
        for at in range(per_slice):
            part = acc[(rep ^ mask) * per_slice + at]
            out_ref[at * block : (at + 1) * block, :] = part.astype(jnp.bfloat16)


def dense_kernel(rep_size, *refs):
    part_refs, refs = refs[:rep_size], refs[rep_size:]
    scaled_ref, inv_ref, weight_ref, bias_ref, cotangent_ref, out_ref, keep_ref, send_ref = refs
    width = scaled_ref.shape[1]
    inv_root = jnp.concatenate([inv_ref[...]] * 2, axis=1)
    sums = [0.0, 0.0]
    for mask, part_ref in enumerate(part_refs):
        sums[mask % 2] += part_ref[...].astype(jnp.float32)
    odd = lax.axis_index("rep") % 2
    agg = jnp.concatenate(
        [jnp.where(odd == 0, sums[0], sums[1]), jnp.where(odd == 0, sums[1], sums[0])], axis=1
    )
    mixed = ((agg + scaled_ref[...].astype(jnp.float32)) * inv_root).astype(jnp.bfloat16)
    pre = jnp.dot(mixed, weight_ref[...], preferred_element_type=jnp.float32) + bias_ref[...]
    square = pre * pre
    bent = jnp.tanh(GELU_C * (pre + 0.044715 * (square * pre)))
    half = 0.5 * (1.0 + bent)
    out_ref[...] = (pre * half).astype(jnp.bfloat16)
    inner = GELU_C * (1.0 + (3 * 0.044715) * square)
    slope = cotangent_ref[...].astype(jnp.float32) * (
        half + 0.5 * pre * ((1.0 - bent) * (1.0 + bent)) * inner
    )
    weight_term = lax.dot_general(
        mixed, slope.astype(jnp.bfloat16), (((0,), (0,)), ((), ())),
        preferred_element_type=jnp.float32,
    )
    bias_term = jnp.sum(slope, axis=0, keepdims=True)
    kept = width // 2
    top, bottom = weight_term[:kept], weight_term[kept:]
    core = lax.axis_index("dom") % 2
    keep_ref[:kept, :] = jnp.where(core == 0, top, bottom)
    send_ref[:kept, :] = jnp.where(core == 0, bottom, top).astype(jnp.bfloat16)
    extra = jnp.broadcast_to(bias_term, (keep_ref.shape[0] - kept, width))
    keep_ref[kept:, :] = extra
    send_ref[kept:, :] = extra.astype(jnp.bfloat16)


def finish_kernel(mine_ref, other_ref, outcome_ref, weight_ref, bias_ref, out_ref):
    kept = weight_ref.shape[0] // 2
    first = lax.axis_index("dom") % 2 == 0
    mine = mine_ref[...].astype(jnp.float32)
    other = other_ref[...].astype(jnp.float32)
    weight_ref[:kept, :] = jnp.where(first, mine[:kept], other[:kept])
    weight_ref[kept:, :] = jnp.where(first, other[:kept], mine[:kept])
    bias_ref[...] = mine[kept : kept + 1]
    out_ref[...] = outcome_ref[...]


def xor_pairs(size, mask):
    return [(at, at ^ mask) for at in range(size)]


def exchange_sum(value, axis, masks):
    size = lax.axis_size(axis)
    while masks:
        now, masks = masks[:2], masks[2:]
        first = lax.ppermute(value, axis, xor_pairs(size, now[0]))
        if len(now) == 1:
            total = value.astype(jnp.float32) + first.astype(jnp.float32)
        else:
            second = lax.ppermute(value, axis, xor_pairs(size, now[1]))
            third = lax.ppermute(value, axis, xor_pairs(size, now[0] ^ now[1]))
            total = (value.astype(jnp.float32) + first.astype(jnp.float32)) + (
                second.astype(jnp.float32) + third.astype(jnp.float32)
            )
        value = total.astype(value.dtype)
    return value


def bits_of(size):
    return [1 << at for at in range(size.bit_length() - 1)]


def on_device(features, degree, tile_row, tile_col, tile_count, tile_live, weight, bias, cotangent):
    row_count, width = features.shape
    dom_size, rep_size = lax.axis_size("dom"), lax.axis_size("rep")
    sections, slots, block = tile_count.shape[1], tile_count.shape[2], tile_count.shape[3]
    block_count = row_count * rep_size // block
    degree_row = degree.reshape(1, row_count)
    bf16, f32 = jnp.bfloat16, jnp.float32
    half = jax.ShapeDtypeStruct((row_count, width // 2), bf16)

    outgoing = local_call(
        lambda *refs: scale_kernel(sections, *refs), "scale",
        (features, degree_row), [HBM] * 2, (half, half), (features, degree_row),
        [pltpu.SemaphoreType.DMA((2,))], 53.375,
    )
    arrived = []
    for flip, part in enumerate(outgoing):
        moves = []
        for dom in range(dom_size):
            plane = dom // sections
            for rep in range(rep_size):
                target = chip_of(plane, plane ^ (flip * (rep_size - 1)), rep, rep_size) * sections + dom % sections
                moves.append((dom * rep_size + rep, target * rep_size + (plane ^ (flip * (rep_size - 1)))))
        arrived.append(lax.ppermute(part, ("dom", "rep"), moves))

    tiles, scaled, inv_root, bias_row = local_call(
        lambda *refs: prepare_kernel(block_count, *refs), "prepare",
        (tile_count, tile_row, tile_col, features, degree_row, bias.reshape(1, width)),
        [VMEM, SMEM, SMEM, VMEM, VMEM, VMEM],
        (
            jax.ShapeDtypeStruct((sections * slots * block + CODE_ROWS, block), bf16),
            jax.ShapeDtypeStruct((row_count, width), bf16),
            jax.ShapeDtypeStruct((row_count, width // 2), f32),
            jax.ShapeDtypeStruct((1, width), f32),
        ),
    )
    their_tiles = lax.ppermute(tiles, "rep", xor_pairs(rep_size, rep_size - 1))

    pieces = [None] * dom_size
    pieces[0] = local_call(
        join_kernel, "join", arrived, [VMEM] * 2,
        jax.ShapeDtypeStruct((2 * row_count, width // 2), bf16),
    )
    for mask in range(2, dom_size, 2):
        pieces[mask] = lax.ppermute(pieces[0], "dom", xor_pairs(dom_size, mask))
    for mask in range(0, dom_size, 2):
        pieces[mask + 1] = lax.ppermute(pieces[mask], "dom", xor_pairs(dom_size, 1))

    partials = local_call(
        lambda *refs: aggregate_kernel(dom_size, rep_size, sections, slots, *refs), "aggregate",
        (tiles, their_tiles, *pieces), [VMEM] * (2 + dom_size),
        (half,) * rep_size,
        (
            jax.ShapeDtypeStruct((dom_size * 2 * row_count // block, block, width // 2), bf16),
            jax.ShapeDtypeStruct((block_count, block, width // 2), f32),
        ),
    )

    parts = [partials[0]]
    for mask in range(1, rep_size):
        parts.append(lax.ppermute(partials[mask], "rep", xor_pairs(rep_size, mask)))

    share = [jax.ShapeDtypeStruct((width // 2 + 16, width), each) for each in (f32, bf16)]
    outcome, keep, send = local_call(
        lambda *refs: dense_kernel(rep_size, *refs), "dense",
        (*parts, scaled, inv_root, weight, bias_row, cotangent),
        [VMEM] * (rep_size + 5),
        (jax.ShapeDtypeStruct((row_count, width), bf16), *share),
    )

    swap = xor_pairs(dom_size, 1)
    mine = (keep + lax.ppermute(send, "dom", swap).astype(f32)).astype(bf16)
    mine = exchange_sum(mine, "dom", bits_of(dom_size)[1:])
    mine = exchange_sum(mine, "rep", bits_of(rep_size))
    other = lax.ppermute(mine, "dom", swap)
    weight_grad, bias_grad, outcome = local_call(
        finish_kernel, "finish", (mine, other, outcome), [VMEM] * 3,
        (
            jax.ShapeDtypeStruct((width, width), f32),
            jax.ShapeDtypeStruct((1, width), f32),
            jax.ShapeDtypeStruct((row_count, width), bf16),
        ),
    )
    return (outcome, weight_grad, bias_grad.reshape(width))


def solution(mesh):
    return jax.shard_map(
        on_device,
        mesh=mesh,
        in_specs=(
            P(("dom", "rep"), None),
            P(("dom", "rep")),
            P("dom", "rep", None),
            P("dom", "rep", None),
            P("dom", "rep", None, None, None),
            P("dom", "rep"),
            P(),
            P(),
            P(("dom", "rep"), None),
        ),
        out_specs=(P(("dom", "rep"), None), P(), P()),
        check_vma=False,
    )
```
